256 devices in a mesh: seq: 16 (over z_hi, x), tp: 16 (over z_lo, y, core).
Axes of the slice: x: 4, y: 4, z: 8 (z_hi: 4, z_lo: 2; z = z_hi * 2 + z_lo), core: 2. Of those that a mesh axis runs over, the one named last changes fastest.
Arguments:
- tokens: bfloat16 [12288, 1152], P('seq', 'tp'), may hold values from -6 to 6
- modulation: float32 [9, 1152], replicated, may hold values from -3 to 3
- spatial_qkv: bfloat16 [3, 1152, 1152], P(None, None, 'tp'), may hold values from -1 to 1
- spatial_out: bfloat16 [1152, 1152], P('tp'), may hold values from -0.1875 to 0.1875
- temporal_qkv: bfloat16 [3, 1152, 1152], P(None, None, 'tp'), may hold values from -1 to 1
- temporal_out: bfloat16 [1152, 1152], P('tp'), may hold values from -0.1875 to 0.1875
- mlp_in: bfloat16 [1152, 4608], P(None, 'tp'), may hold values from -0.1875 to 0.1875
- mlp_out: bfloat16 [4608, 1152], P('tp'), may hold values from -0.09375 to 0.09375
Outputs:
- result: bfloat16 [12288, 1152], P('seq', 'tp')
The draws below stay inside these ranges and needn't reach their ends.
All inputs are finite; a program needn't handle non-finite values.
Results may differ from the reference program's by a relative error of at most 0.035.
Values may be sent and summed in bfloat16 or wider, within the bound.
A program may use at most 64 MiB of HBM per device.

```python
import jax
import jax.numpy as jnp
from jax import lax

D = 1152
FF = 4608
POS = 768
HD = 72
FRAMES = 16
TOKENS = 12288
N_TP = 16


def drawn_projections(key):
    entries = jax.random.normal(key, (3, D, D), jnp.float32)
    return jnp.clip(entries, -6.0, 6.0) * D ** (-0.5)


def draw_spatial_qkv(key, part):
    key = jax.random.fold_in(key, 11)
    drawn = drawn_projections(key)
    return jnp.clip(drawn, -1.0, 1.0).astype(jnp.bfloat16)


def draw_temporal_qkv(key, part):
    key = jax.random.fold_in(key, 12)
    drawn = drawn_projections(key)
    return jnp.clip(drawn, -1.0, 1.0).astype(jnp.bfloat16)


def block_levels(key, shape, shards, least, high):
    factor_of, own = 1.0, jax.random.fold_in(key, 6)
    for position, shards_of in shards:
        heights = jnp.exp(jax.random.uniform(jax.random.fold_in(own, position), (shards_of,), jnp.float32, least / len(shards), high / len(shards)))
        factor_of = factor_of * jnp.repeat(heights, shape[position] // shards_of).reshape([-1 if axis == position else 1 for axis in range(len(shape))])
    return factor_of


def scatter_about(stream_key, dims, scale, reach, pieces=(), held_as=jnp.bfloat16):
    gain = block_levels(stream_key, dims, pieces, -0.22, 0.18) if pieces else 1.0
    array = jax.random.normal(stream_key, dims, jnp.float32) * scale * gain
    return jnp.minimum(jnp.maximum(array, -reach), reach).astype(held_as)


def setup_inputs(seed: int = 0) -> dict:
    splits = jax.random.split(jax.random.key(seed), 9)
    return {
        "tokens": scatter_about(splits[0], (TOKENS, D), 1.0, 6.0, ((0, 16), (1, 16))),
        "modulation": scatter_about(splits[1], (9, D), 0.5, 3.0, (), jnp.float32),
        "spatial_qkv": draw_spatial_qkv(jax.random.fold_in(splits[8], 71), 0),
        "spatial_out": scatter_about(splits[3], (D, D), D ** -0.5, 0.1875, ((0, 16),)),
        "temporal_qkv": draw_temporal_qkv(jax.random.fold_in(splits[8], 71), 0),
        "temporal_out": scatter_about(splits[5], (D, D), D ** -0.5, 0.1875, ((0, 16),)),
        "mlp_in": scatter_about(splits[6], (D, FF), D ** -0.5, 0.1875, ((1, 16),)),
        "mlp_out": scatter_about(splits[7], (FF, D), FF ** -0.5, 0.09375, ((0, 16),)),
    }


norm_eps = 1e-06

def modulated(inputs, shift_row, scale_row):
    as_float = inputs.astype(jnp.float32)
    average = lax.optimization_barrier(jnp.mean(as_float, axis=-1, keepdims=True))
    centred = as_float - average
    variance = lax.optimization_barrier(jnp.mean(centred * centred, axis=-1, keepdims=True))
    normed = centred * lax.rsqrt(variance + norm_eps)
    return (normed * (1.0 + scale_row) + shift_row).astype(jnp.bfloat16)

def project_three(normed, weights):
    return [jnp.dot(normed, weights[proj_index], preferred_element_type=jnp.float32).astype(jnp.bfloat16) for proj_index in range(3)]

def spatial_mix(queries, keys_in, values_in):
    row_count = queries.shape[0]
    heads_here = queries.shape[1] // HD

    def split_heads(tensor):
        return tensor.reshape(row_count, heads_here, HD).transpose(1, 0, 2)

    def one_head(triple):
        query_h, key_h, value_h = triple
        scores = lax.dot_general(query_h, key_h, (((1,), (1,)), ((), ())), preferred_element_type=jnp.float32) * HD ** (-0.5)
        row_top = lax.optimization_barrier(jnp.max(scores, axis=1, keepdims=True))
        raised = jnp.exp(scores - row_top)
        weights = (raised / lax.optimization_barrier(jnp.sum(raised, axis=1, keepdims=True))).astype(jnp.bfloat16)
        return jnp.dot(weights, value_h, preferred_element_type=jnp.float32).astype(jnp.bfloat16)
    mixture = lax.map(one_head, (split_heads(queries), split_heads(keys_in), split_heads(values_in)))
    return mixture.transpose(1, 0, 2).reshape(row_count, heads_here * HD)

def temporal_mix(queries, keys_in, values_in):
    frames_n, places, full_width = queries.shape
    head_shape = (frames_n, places, full_width // HD, HD)
    query_f = queries.reshape(head_shape).astype(jnp.float32)
    key_f = keys_in.reshape(head_shape).astype(jnp.float32)
    value_f = values_in.reshape(head_shape).astype(jnp.float32)
    scores = jnp.einsum('fphd,gphd->phfg', query_f, key_f) * HD ** (-0.5)
    row_top = lax.optimization_barrier(jnp.max(scores, axis=-1, keepdims=True))
    raised = jnp.exp(scores - row_top)
    weights = (raised / lax.optimization_barrier(jnp.sum(raised, axis=-1, keepdims=True))).astype(jnp.bfloat16)
    mixture = jnp.einsum('phfg,gphd->fphd', weights.astype(jnp.float32), value_f)
    return mixture.astype(jnp.bfloat16).reshape(frames_n, places, full_width)

def grouped_sum(mixture, weight_rows):
    group_width = mixture.shape[-1] // N_TP
    summed = jnp.zeros((mixture.shape[0], weight_rows.shape[1]), jnp.float32)
    for group_index in range(N_TP):
        low = group_index * group_width
        group_term = jnp.dot(mixture[:, low:low + group_width], weight_rows[low:low + group_width], preferred_element_type=jnp.float32)
        summed = summed + group_term.astype(jnp.bfloat16).astype(jnp.float32)
    return summed

def reference(tokens, modulation, spatial_qkv, spatial_out, temporal_qkv, temporal_out, mlp_in, mlp_out):
    frames_all = tokens.reshape(FRAMES, POS, D)

    def spatial_frame(one_frame):
        normed = modulated(one_frame, modulation[0], modulation[1])
        queries, keys_in, values_in = project_three(normed, spatial_qkv)
        attended = grouped_sum(spatial_mix(queries, keys_in, values_in), spatial_out)
        return (one_frame.astype(jnp.float32) + modulation[2] * attended).astype(jnp.bfloat16)
    after_spatial = lax.map(spatial_frame, frames_all)
    normed = modulated(after_spatial, modulation[3], modulation[4])
    queries, keys_in, values_in = project_three(normed, temporal_qkv)
    mixture = temporal_mix(queries, keys_in, values_in)
    attended = grouped_sum(mixture.reshape(TOKENS, D), temporal_out).reshape(FRAMES, POS, D)
    after_temporal = (after_spatial.astype(jnp.float32) + modulation[5] * attended).astype(jnp.bfloat16)

    def mlp_frame(one_frame):
        normed_mlp = modulated(one_frame, modulation[6], modulation[7])
        hidden = jax.nn.gelu(jnp.dot(normed_mlp, mlp_in, preferred_element_type=jnp.float32), approximate=True).astype(jnp.bfloat16)
        return (one_frame.astype(jnp.float32) + modulation[8] * grouped_sum(hidden, mlp_out)).astype(jnp.bfloat16)
    return lax.map(mlp_frame, after_temporal).reshape(TOKENS, D)
```

```python
import jax
import jax.numpy as jnp
from jax import lax
from jax.experimental import pallas as pl
from jax.experimental.pallas import tpu as pltpu
from jax.sharding import PartitionSpec as P

HD = 72
D = 1152
N = 16
ROWS = 768
BLK = 48
FFL = 288
PADW = 80
EPS = 1e-06
SCALE = HD ** (-0.5)
BF = jnp.bfloat16
F32 = jnp.float32


def remote(src, dst, send_sem, recv_sem, device):
    return pltpu.make_async_remote_copy(
        src_ref=src,
        dst_ref=dst,
        send_sem=send_sem,
        recv_sem=recv_sem,
        device_id=device,
        device_id_type=pl.DeviceIdType.MESH,
    )


def modulated(rows, shift, scale):
    average = jnp.mean(rows, axis=-1, keepdims=True)
    centred = rows - average
    variance = jnp.mean(centred * centred, axis=-1, keepdims=True)
    return (centred * lax.rsqrt(variance + EPS) * (1.0 + scale) + shift).astype(BF)


class Gather:
    def __init__(self, slot, send, recv, pos):
        self.slot, self.send, self.recv, self.pos = slot, send, recv, pos
        self.sent = 0
        self.pending = []
        s, z, y, c = pos
        self.up = lax.rem(y + 1 + 2 * c, 4)
        self.down = lax.rem(y + 3 - 2 * c, 4)
        self.far = lax.rem(y + 2, 4)

    def index(self, z, y, c):
        return z * 8 + y * 2 + c

    def push(self, origin, target):
        ref = self.slot(origin)
        s = self.pos[0]
        copy = remote(ref, ref, self.send.at[self.sent], self.recv.at[origin], (s, target))
        copy.start()
        self.sent += 1
        self.pending.append(copy)

    def await_block(self, origin):
        ref = self.slot(origin)
        s, z, y, c = self.pos
        remote(
            ref, ref, self.send.at[0], self.recv.at[origin], (s, self.index(z, y, 1 - c))
        ).wait_recv()

    def p0(self):
        s, z, y, c = self.pos
        own = self.index(z, y, c)
        self.push(own, self.index(1 - z, y, c))
        self.push(own, self.index(z, self.up, c))
        self.push(own, self.index(z, self.down, c))
        self.push(own, self.index(z, y, 1 - c))

    def p1(self):
        s, z, y, c = self.pos
        block = self.index(1 - z, y, c)
        self.await_block(block)
        self.push(block, self.index(z, self.up, c))
        self.push(block, self.index(z, self.down, c))
        self.push(block, self.index(z, y, 1 - c))

    def ring(self, zz):
        s, z, y, c = self.pos
        block = self.index(zz, self.down, c)
        self.await_block(block)
        self.push(block, self.index(z, self.up, c))
        self.push(block, self.index(z, y, 1 - c))
        block = self.index(zz, self.up, c)
        self.await_block(block)
        self.push(block, self.index(z, y, 1 - c))

    def p2(self):
        self.ring(self.pos[1])

    def p3(self):
        self.ring(1 - self.pos[1])

    def p4(self):
        s, z, y, c = self.pos
        for zz in (z, 1 - z):
            block = self.index(zz, self.far, c)
            self.await_block(block)
            self.push(block, self.index(z, y, 1 - c))

    def p5(self):
        s, z, y, c = self.pos
        for zz in (z, 1 - z):
            for yy in (y, self.down, self.up, self.far):
                self.await_block(self.index(zz, yy, 1 - c))

    def finish(self):
        for copy in self.pending:
            copy.wait_send()


def kernel(
    tok, mod, wqkv1, wout1, wqkv2, wout2, wmi, wmo, out,
    tokr, tokf, g1, g2, g3, wo1, wo2, wc1, wc2,
    qb, kb, vb, o1b, o1f, qkvb, o2b, o2r, xb, acc,
    rs_send, rs_a, own_sum, rs_b, rs_c, rs_d, rs_e, mid_b, mid_c, mid_d, mid_e,
    res_s, res_r,
    tr_s, tr_r, tf_s, tf_r, o1_s, o1_r, o2_s, o2_r, re_s, re_r,
    g1_s, g1_r, g2_s, g2_r, g3_s, g3_r, w1_s, w1_r, w2_s, w2_r,
    ra_s, ra_r, rb_s, rb_r, rc_s, rc_r, rd_s, rd_r, re2_s, re2_r,
):
    s = lax.axis_index("seq")
    t = lax.axis_index("tp")
    z = lax.div(t, 8)
    y = lax.rem(lax.div(t, 2), 4)
    c = lax.rem(t, 2)
    pos = (s, z, y, c)
    diagonal = s == t

    def rows_of(i):
        return pl.ds(pl.multiple_of(i * BLK, BLK), BLK)

    barrier = pltpu.get_barrier_semaphore()

    def signal(dev):
        pl.semaphore_signal(barrier, inc=1, device_id=dev, device_id_type=pl.DeviceIdType.MESH)

    @pl.loop(1, N)
    def _(i):
        signal((s, lax.rem(t + i, N)))
        signal((lax.rem(s + i, N), s))
        signal((t, lax.rem(t + i, N)))

    @pl.when(jnp.logical_not(diagonal))
    def _():
        signal((s, s))
        signal((t, t))

    pl.semaphore_wait(barrier, 45 + jnp.where(diagonal, 0, 2))

    def tok_copy(i):
        peer = lax.rem(t + i, N)
        return remote(tok.at[rows_of(peer)], tokr.at[t], tr_s.at[i], tr_r.at[t], (s, peer))

    @pl.loop(1, N)
    def _(i):
        tok_copy(i).start()

    def far_copy(src, dst, ss, rs, i):
        r = lax.rem(s + i, N)
        return remote(src.at[rows_of(r)], dst.at[t], ss.at[i], rs.at[t], (r, s))

    def far_start(src, dst, ss, rs):
        @pl.when(jnp.logical_not(diagonal))
        def _():
            far_copy(src, dst, ss, rs, 0).start()

        @pl.when(diagonal)
        def _():
            dst[t] = src[rows_of(s), :]

        @pl.loop(1, N)
        def _(i):
            far_copy(src, dst, ss, rs, i).start()

    def far_wait_recv(src, dst, ss, rs):
        @pl.when(jnp.logical_not(diagonal))
        def _():
            remote(src.at[rows_of(0)], dst.at[t], ss.at[0], rs.at[t], (s, s)).wait_recv()

        @pl.loop(1, N)
        def _(i):
            k = lax.rem(t + i, N)
            remote(src.at[rows_of(0)], dst.at[k], ss.at[0], rs.at[k], (t, k)).wait_recv()

    def far_wait_send(src, dst, ss, rs):
        @pl.when(jnp.logical_not(diagonal))
        def _():
            far_copy(src, dst, ss, rs, 0).wait_send()

        @pl.loop(1, N)
        def _(i):
            far_copy(src, dst, ss, rs, i).wait_send()

    far_start(tok, tokf, tf_s, tf_r)
    tokr[t] = tok[rows_of(t), :]

    for j in range(3):
        wc1[:, j * HD:(j + 1) * HD] = wqkv1[j]
    for j in range(3):
        wc2[:, j * HD:(j + 1) * HD] = wqkv2[j]
    for w_in, w_all in ((wout1, wo1), (wout2, wo2)):
        w_all[t, 0:HD, :] = w_in[...]
        w_all[t, HD:PADW, :] = jnp.zeros((PADW - HD, D), BF)
    lanes = lax.broadcasted_iota(jnp.int32, (ROWS, 128), 1)
    vb[...] = jnp.where(lanes == HD, 1.0, 0.0).astype(BF)

    @pl.loop(1, N)
    def _(i):
        k = lax.rem(t + i, N)
        remote(tok.at[rows_of(0)], tokr.at[k], tr_s.at[0], tr_r.at[k], (s, k)).wait_recv()

    def side_by_side(blocks):
        for k in range(N):
            xb[:, k * HD:(k + 1) * HD] = blocks[k].astype(F32)

    side_by_side(tokr)

    def gather_of(buf, send, recv):
        return Gather(lambda i: buf.at[rows_of(i)], send, recv, pos)

    ga1 = gather_of(g1, g1_s, g1_r)
    g1[rows_of(t), :] = modulated(xb[...], mod[0:1, :], mod[1:2, :])
    ga1.p0()
    ga1.p1()
    ga1.p2()
    ga1.p3()
    ga1.p4()
    gw1 = Gather(lambda i: wo1.at[i], w1_s, w1_r, pos)
    gw1.p0()
    ga1.p5()

    @pl.loop(0, 3)
    def _(i):
        rows = pl.ds(pl.multiple_of(i * 256, 256), 256)
        r = jnp.dot(g1[rows, :], wc1[...], preferred_element_type=F32)
        qb[rows, :] = r[:, 0:HD].astype(BF)
        kb[rows, :] = r[:, HD:2 * HD].astype(BF)
        vb[rows, 0:HD] = r[:, 2 * HD:3 * HD].astype(BF)

    gw1.p1()
    gw1.p2()

    @pl.loop(0, 3)
    def _(i):
        rows = pl.ds(pl.multiple_of(i * 256, 256), 256)
        scores = lax.dot_general(
            qb[rows, :], kb[...], (((1,), (1,)), ((), ())), preferred_element_type=F32
        )
        top = jnp.max(scores, axis=1, keepdims=True)
        raised = jnp.exp((scores - top) * SCALE).astype(BF)
        mixed = jnp.dot(raised, vb[...], preferred_element_type=F32)
        o1b[rows, :] = (mixed[:, 0:HD] / mixed[:, HD:HD + 1]).astype(BF)

    far_start(o1b, o1f, o1_s, o1_r)
    gw1.p3()
    gw1.p4()
    far_wait_recv(tok, tokf, tf_s, tf_r)
    side_by_side(tokf)
    far_wait_recv(o1b, o1f, o1_s, o1_r)
    gw1.p5()

    def project(blocks, weights):
        acc[...] = jnp.zeros((BLK, D), F32)

        @pl.loop(0, N)
        def _(k):
            term = jnp.dot(blocks[k], weights[k, 0:HD, :], preferred_element_type=F32)
            acc[...] += term.astype(BF).astype(F32)

    project(o1f, wo1)
    x1 = (xb[...] + mod[2:3, :] * acc[...]).astype(BF).astype(F32)
    xb[...] = x1
    ga2 = gather_of(g2, g2_s, g2_r)
    g2[rows_of(t), :] = modulated(x1, mod[3:4, :], mod[4:5, :])
    ga2.p0()
    ga2.p1()
    ga2.p2()
    ga2.p3()
    ga2.p4()
    gw2 = Gather(lambda i: wo2.at[i], w2_s, w2_r, pos)
    gw2.p0()
    ga2.p5()

    @pl.loop(0, 3)
    def _(i):
        rows = pl.ds(pl.multiple_of(i * 256, 256), 256)
        r = jnp.dot(g2[rows, :], wc2[...], preferred_element_type=F32)
        qkvb[rows, :] = r.astype(BF)

    gw2.p1()
    gw2.p2()

    same = lax.rem(lax.broadcasted_iota(jnp.int32, (256, 256), 0), 16) == lax.rem(
        lax.broadcasted_iota(jnp.int32, (256, 256), 1), 16
    )
    for grp in range(3):
        part = jnp.concatenate(
            [qkvb[f * BLK + grp * 16:f * BLK + grp * 16 + 16, :] for f in range(N)], axis=0
        )
        q, k, v = part[:, 0:HD], part[:, HD:2 * HD], part[:, 2 * HD:3 * HD]
        scores = lax.dot_general(q, k, (((1,), (1,)), ((), ())), preferred_element_type=F32)
        scores = jnp.where(same, scores, -1e30)
        top = jnp.max(scores, axis=1, keepdims=True)
        raised = jnp.where(same, jnp.exp((scores - top) * SCALE), 0.0)
        weights = (raised / jnp.sum(raised, axis=1, keepdims=True)).astype(BF)
        mixed = jnp.dot(weights, v, preferred_element_type=F32).astype(BF)
        for f in range(N):
            o2b[f * BLK + grp * 16:f * BLK + grp * 16 + 16, :] = mixed[f * 16:f * 16 + 16, :]

    def o2_copy(i):
        peer = lax.rem(t + i, N)
        return remote(o2b.at[rows_of(peer)], o2r.at[t], o2_s.at[i], o2_r.at[t], (s, peer))

    @pl.loop(1, N)
    def _(i):
        o2_copy(i).start()

    o2r[t] = o2b[rows_of(t), :]
    gw2.p3()
    gw2.p4()

    @pl.loop(1, N)
    def _(i):
        k = lax.rem(t + i, N)
        remote(o2b.at[rows_of(0)], o2r.at[k], o2_s.at[0], o2_r.at[k], (s, k)).wait_recv()

    gw2.p5()
    project(o2r, wo2)
    x2 = (xb[...] + mod[5:6, :] * acc[...]).astype(BF).astype(F32)
    xb[...] = x2
    ga3 = gather_of(g3, g3_s, g3_r)
    g3[rows_of(t), :] = modulated(x2, mod[6:7, :], mod[7:8, :])
    ga3.p0()
    ga3.p1()
    ga3.p2()
    ga3.p3()
    ga3.p4()
    ga3.p5()

    def mlp(zz, cc):
        rows = jnp.concatenate([g3[rows_of(zz * 8 + yy * 2 + cc), :] for yy in range(4)], axis=0)
        hidden = jax.nn.gelu(
            jnp.dot(rows, wmi[...], preferred_element_type=F32), approximate=True
        ).astype(BF)
        return jnp.dot(hidden, wmo[...], preferred_element_type=F32)

    partner = (s, z * 8 + y * 2 + 1 - c)

    def ra_copy(j):
        return remote(rs_send.at[j], rs_a.at[j], ra_s.at[j], ra_r.at[j], partner)

    @pl.loop(0, 2)
    def _(zz):
        r = mlp(zz, 1 - c)
        for yy in range(4):
            rs_send[zz * 4 + yy] = r[yy * BLK:(yy + 1) * BLK, :].astype(BF)
            ra_copy(zz * 4 + yy).start()

    @pl.loop(0, 2)
    def _(zz):
        r = mlp(zz, c)
        for yy in range(4):
            own_sum[zz * 4 + yy] = r[yy * BLK:(yy + 1) * BLK, :]

    up = lax.rem(y + 1 + 2 * c, 4)
    down = lax.rem(y + 3 - 2 * c, 4)
    far = lax.rem(y + 2, 4)
    to_up = (s, z * 8 + up * 2 + c)
    to_down = (s, z * 8 + down * 2 + c)
    to_z = (s, (1 - z) * 8 + y * 2 + c)

    def chip_sum(zz, yy):
        ra_copy(zz * 4 + yy).wait_recv()
        return own_sum[zz * 4 + yy] + rs_a[zz * 4 + yy].astype(F32)

    def rb_copy(zz):
        return remote(mid_b.at[zz], rs_b.at[zz], rb_s.at[zz], rb_r.at[zz], to_up)

    def rc_copy(zz):
        return remote(mid_c.at[zz], rs_c.at[zz], rc_s.at[zz], rc_r.at[zz], to_down)

    def rd_copy(zz):
        return remote(mid_d.at[zz], rs_d.at[zz], rd_s.at[zz], rd_r.at[zz], to_up)

    for zz in range(2):
        mid_b[zz] = chip_sum(zz, far).astype(BF)
        rb_copy(zz).start()
    for zz in range(2):
        mid_c[zz] = chip_sum(zz, down).astype(BF)
        rc_copy(zz).start()
    for zz in range(2):
        r = chip_sum(zz, up)
        rb_copy(zz).wait_recv()
        mid_d[zz] = (r + rs_b[zz].astype(F32)).astype(BF)
        rd_copy(zz).start()
    for zz in range(2):
        own_sum[zz * 4 + y] = chip_sum(zz, y)
    for zz in range(2):
        rc_copy(zz).wait_recv()
        rd_copy(zz).wait_recv()
    mid_e[...] = (
        own_sum[(1 - z) * 4 + y] + rs_c[1 - z].astype(F32) + rs_d[1 - z].astype(F32)
    ).astype(BF)
    re_copy = remote(mid_e, rs_e, re2_s, re2_r, to_z)
    re_copy.start()
    mine = own_sum[z * 4 + y] + rs_c[z].astype(F32) + rs_d[z].astype(F32)
    re_copy.wait_recv()
    total = mine + rs_e[...].astype(F32)
    result = (xb[...] + mod[8:9, :] * total).astype(BF)
    for k in range(N):
        res_s[k] = result[:, k * HD:(k + 1) * HD]

    def res_copy(i):
        k = lax.rem(t + i, N)
        return remote(res_s.at[k], res_r.at[rows_of(s)], re_s.at[i], re_r.at[s], (t, k))

    @pl.when(jnp.logical_not(diagonal))
    def _():
        res_copy(0).start()

    @pl.when(diagonal)
    def _():
        res_r[rows_of(s), :] = res_s[t]

    @pl.loop(1, N)
    def _(i):
        res_copy(i).start()

    @pl.loop(1, N)
    def _(i):
        tok_copy(i).wait_send()
        o2_copy(i).wait_send()

    far_wait_send(tok, tokf, tf_s, tf_r)
    far_wait_send(o1b, o1f, o1_s, o1_r)
    for g in (ga1, ga2, ga3, gw1, gw2):
        g.finish()

    @pl.loop(0, 8)
    def _(j):
        ra_copy(j).wait_send()

    for zz in range(2):
        rb_copy(zz).wait_send()
        rc_copy(zz).wait_send()
        rd_copy(zz).wait_send()
    re_copy.wait_send()

    @pl.when(jnp.logical_not(diagonal))
    def _():
        res_copy(0).wait_send()
        remote(res_s.at[0], res_r.at[rows_of(s)], re_s.at[0], re_r.at[s], (s, s)).wait_recv()

    @pl.loop(1, N)
    def _(i):
        res_copy(i).wait_send()
        k = lax.rem(s + i, N)
        remote(res_s.at[0], res_r.at[rows_of(k)], re_s.at[0], re_r.at[k], (k, s)).wait_recv()

    out[...] = res_r[...]


def per_device(tokens, modulation, spatial_qkv, spatial_out, temporal_qkv, temporal_out, mlp_in, mlp_out):
    vm = pltpu.VMEM
    dma = pltpu.SemaphoreType.DMA
    scratch = [
        vm((N, BLK, HD), BF),
        vm((N, BLK, HD), BF),
        vm((ROWS, D), BF),
        vm((ROWS, D), BF),
        vm((ROWS, D), BF),
        vm((N, PADW, D), BF),
        vm((N, PADW, D), BF),
        vm((D, 3 * HD), BF),
        vm((D, 3 * HD), BF),
        vm((ROWS, HD), BF),
        vm((ROWS, HD), BF),
        vm((ROWS, 128), BF),
        vm((ROWS, HD), BF),
        vm((N, BLK, HD), BF),
        vm((ROWS, 3 * HD), BF),
        vm((ROWS, HD), BF),
        vm((N, BLK, HD), BF),
        vm((BLK, D), F32),
        vm((BLK, D), F32),
        vm((8, BLK, D), BF),
        vm((8, BLK, D), BF),
        vm((8, BLK, D), F32),
        vm((2, BLK, D), BF),
        vm((2, BLK, D), BF),
        vm((2, BLK, D), BF),
        vm((BLK, D), BF),
        vm((2, BLK, D), BF),
        vm((2, BLK, D), BF),
        vm((2, BLK, D), BF),
        vm((BLK, D), BF),
        vm((N, BLK, HD), BF),
        vm((ROWS, HD), BF),
    ]
    scratch += [dma((N,))] * 20
    scratch += [dma((8,)), dma((8,))] + [dma((2,))] * 6 + [dma, dma]
    return pl.pallas_call(
        kernel,
        out_shape=jax.ShapeDtypeStruct((ROWS, HD), BF),
        in_specs=[pl.BlockSpec(memory_space=pltpu.VMEM)] * 8,
        out_specs=pl.BlockSpec(memory_space=pltpu.VMEM),
        scratch_shapes=scratch,
        compiler_params=pltpu.CompilerParams(
            collective_id=0, has_side_effects=True, vmem_limit_bytes=50 * 1024 * 1024
        ),
        cost_estimate=pl.CostEstimate(
            flops=2_300_000_000, bytes_accessed=4_000_000, transcendentals=1_000_000
        ),
    )(tokens, modulation, spatial_qkv, spatial_out, temporal_qkv, temporal_out, mlp_in, mlp_out)


def solution(mesh):
    return jax.shard_map(
        per_device,
        mesh=mesh,
        in_specs=(
            P("seq", "tp"),
            P(),
            P(None, None, "tp"),
            P("tp", None),
            P(None, None, "tp"),
            P("tp", None),
            P(None, "tp"),
            P("tp", None),
        ),
        out_specs=P("seq", "tp"),
        check_vma=False,
    )
```

```python
import jax
import jax.numpy as jnp
from jax import lax
from jax.experimental import pallas as pl
from jax.experimental.pallas import tpu as pltpu
from jax.sharding import PartitionSpec as P

HD = 72
D = 1152
N = 16
ROWS = 768
BLK = 48
FFL = 288
PADW = 80
CUT = 48
SHARE = 80
EPS = 1e-06
SCALE = HD ** (-0.5)
BF = jnp.bfloat16
F32 = jnp.float32


def remote(src, dst, send_sem, recv_sem, device):
    return pltpu.make_async_remote_copy(
        src_ref=src,
        dst_ref=dst,
        send_sem=send_sem,
        recv_sem=recv_sem,
        device_id=device,
        device_id_type=pl.DeviceIdType.MESH,
    )


def dot_nt(a, b):
    return lax.dot_general(a, b, (((1,), (1,)), ((), ())), preferred_element_type=F32)


def modulated(rows, shift, scale):
    average = jnp.mean(rows, axis=-1, keepdims=True)
    centred = rows - average
    variance = jnp.mean(centred * centred, axis=-1, keepdims=True)
    return (centred * lax.rsqrt(variance + EPS) * (1.0 + scale) + shift).astype(BF)


class Copies:
    def __init__(self, send):
        self.send = send
        self.started = []

    def push(self, src, dst, recv, device):
        copy = remote(src, dst, self.send.at[len(self.started)], recv, device)
        copy.start()
        self.started.append(copy)

    def finish(self):
        for copy in self.started:
            copy.wait_send()


class Place:
    def __init__(self):
        self.s = lax.axis_index("seq")
        self.t = lax.axis_index("tp")
        self.z = lax.div(self.t, 8)
        self.y = lax.rem(lax.div(self.t, 2), 4)
        self.c = lax.rem(self.t, 2)
        self.zh = lax.div(self.s, 4)
        self.x = lax.rem(self.s, 4)
        self.up = lax.rem(self.y + 1, 4)
        self.down = lax.rem(self.y + 3, 4)
        self.far = lax.rem(self.y + 2, 4)

    def at(self, z, y, c):
        return z * 8 + y * 2 + c

    def dev(self, z, y, c):
        return (self.s, self.at(z, y, c))

    def partner(self):
        return self.dev(self.z, self.y, 1 - self.c)

    def z_inner(self):
        return self.dev(1 - self.z, self.y, self.c)

    def z_outer(self):
        zh = lax.rem(self.zh + jnp.where(self.z == 1, 1, 3), 4)
        return (zh * 4 + self.x, self.at(1 - self.z, self.y, self.c))


class Gather:
    def __init__(self, buf, send, recv, at, planes, chunks):
        self.buf, self.recv, self.p, self.planes, self.chunks = buf, recv, at, planes, chunks
        self.rows = BLK // chunks
        self.copies = Copies(send)

    def slot(self, o, k):
        if self.planes == 1:
            o = lax.rem(o, 8)
        return self.buf.at[pl.ds(pl.multiple_of(o * BLK + k * self.rows, self.rows), self.rows)]

    def sem(self, o, k):
        return self.recv.at[o, k]

    def push(self, o, k, device):
        ref = self.slot(o, k)
        self.copies.push(ref, ref, self.sem(o, k), device)

    def arrive(self, o, k):
        ref = self.slot(o, k)
        remote(ref, ref, self.copies.send.at[0], self.sem(o, k), self.p.partner()).wait_recv()

    def start(self):
        p = self.p
        for k in range(self.chunks):
            if self.planes == 2:
                self.push(p.t, k, p.z_inner())
            for yy in (p.up, p.down, p.far):
                self.push(p.t, k, p.dev(p.z, yy, p.c))
        for k in range(self.chunks):
            self.push(p.t, k, p.partner())

    def forward(self):
        p = self.p
        if self.planes == 1:
            return
        for k in range(self.chunks):
            o = p.at(1 - p.z, p.y, p.c)
            self.arrive(o, k)
            for yy in (p.up, p.down):
                self.push(o, k, p.dev(p.z, yy, p.c))
            self.push(o, k, p.partner())
        for k in range(self.chunks):
            o = p.at(p.z, p.far, p.c)
            self.arrive(o, k)
            self.push(o, k, p.z_inner())
            self.push(o, k, p.partner())

    def relay(self):
        p = self.p
        near = (p.up, p.down) if self.planes == 2 else (p.up, p.down, p.far)
        for k in range(self.chunks):
            for yy in near:
                o = p.at(p.z, yy, p.c)
                self.arrive(o, k)
                self.push(o, k, p.partner())
        if self.planes == 2:
            for k in range(self.chunks):
                for yy in (p.up, p.down, p.far):
                    o = p.at(1 - p.z, yy, p.c)
                    self.arrive(o, k)
                    self.push(o, k, p.partner())

    def complete(self):
        p = self.p
        for zz in (p.z, 1 - p.z)[: self.planes]:
            for yy in (p.y, p.up, p.down, p.far):
                for k in range(self.chunks):
                    self.arrive(p.at(zz, yy, 1 - p.c), k)


class WeightGather:
    def __init__(self, buf, send, recv, at):
        self.buf, self.recv, self.p = buf, recv, at
        self.copies = Copies(send)

    def part(self, o, h):
        return self.buf.at[o, pl.ds(0, CUT)] if h == 0 else self.buf.at[o, pl.ds(CUT, PADW - CUT)]

    def halves(self, o):
        p = self.p
        for h, device in ((0, p.z_inner()), (1, p.z_outer())):
            ref = self.part(o, h)
            self.copies.push(ref, ref, self.recv.at[o, h], device)

    def whole(self, o, device):
        ref = self.buf.at[o]
        self.copies.push(ref, ref, self.recv.at[o, 0], device)

    def arrive(self, o):
        ref = self.buf.at[o]
        remote(ref, ref, self.copies.send.at[0], self.recv.at[o, 0], self.p.partner()).wait_recv()

    def start_z(self):
        self.halves(self.p.t)

    def start_y(self):
        p = self.p
        for yy in (p.up, p.down, p.far):
            self.whole(p.t, p.dev(p.z, yy, p.c))
        self.whole(p.t, p.partner())

    def forward(self):
        p = self.p
        for yy in (p.up, p.down, p.far):
            o = p.at(p.z, yy, p.c)
            self.arrive(o)
            self.halves(o)
            self.whole(o, p.partner())

    def relay(self):
        p = self.p
        for yy in (p.y, p.up, p.down, p.far):
            o = p.at(1 - p.z, yy, p.c)
            for h in range(2):
                ref = self.part(o, h)
                remote(ref, ref, self.copies.send.at[0], self.recv.at[o, h], p.partner()).wait_recv()
            self.whole(o, p.partner())

    def complete(self):
        p = self.p
        for zz in (p.z, 1 - p.z):
            for yy in (p.y, p.up, p.down, p.far):
                self.arrive(p.at(zz, yy, 1 - p.c))


def kernel(
    tok_t, mod, wqkv1, wout1, wqkv2, wout2, wmi, wmo, out_t,
    tok, tokr, tokf, g1, g2, g3, wo1, wo2, wc1, wc2, wia, woa,
    qb, kb, vb, o1b, o1f, qkvb, o2b, o2r, xb, xp,
    rs_send, rs_a, own_sum, mid, rs_y, res_s, res_r,
    known_x, known_z,
    tr_s, tr_r, tf_s, tf_r, o1_s, o1_r, o2_s, o2_r, re_s, re_r,
    g1_s, g1_r, g2_s, g2_r, g3_s, g3_r, w1_s, w1_r, w2_s, w2_r, wm_s, wm_r, wl_s,
    ra_s, ra_r, ry_s, ry_r,
):
    p = Place()
    s, t = p.s, p.t
    frame = jnp.bitwise_xor(s, t)
    origin = t == 0

    def rows_of(i):
        return pl.ds(pl.multiple_of(i * BLK, BLK), BLK)

    def tell(sem, dev):
        pl.semaphore_signal(sem, inc=1, device_id=dev, device_id_type=pl.DeviceIdType.MESH)

    barrier = pltpu.get_barrier_semaphore()
    x_peers = [(p.zh * 4 + lax.rem(p.x + j, 4), t) for j in (1, 2, 3)]
    z_peers = [(lax.rem(p.zh + j, 4) * 4 + p.x, t) for j in (1, 2, 3)]

    for dev in x_peers + z_peers + [p.z_outer()]:
        tell(barrier, dev)

    @pl.loop(1, N)
    def _(i):
        tell(barrier, (s, lax.rem(t + i, N)))

    tok[...] = jnp.transpose(tok_t[...].astype(F32)).astype(BF)
    pl.semaphore_wait(barrier, 22)

    def tok_copy(i):
        peer = lax.rem(t + i, N)
        return remote(tok.at[rows_of(peer)], tokr.at[t], tr_s.at[i], tr_r.at[t], (s, peer))

    @pl.loop(1, N)
    def _(i):
        tok_copy(i).start()

    tokr[t] = tok[rows_of(t), :]
    for dev in x_peers:
        tell(known_x, dev)

    local = [
        pltpu.make_async_copy(wmi, wia.at[0], wl_s.at[0]),
        pltpu.make_async_copy(wmo, woa.at[0], wl_s.at[1]),
    ]
    for copy in local:
        copy.start()
    gw1 = WeightGather(wo1, w1_s, w1_r, p)
    gw2 = WeightGather(wo2, w2_s, w2_r, p)
    for w_in, w_all in ((wout1, wo1), (wout2, wo2)):
        w_all[t, 0:HD, :] = w_in[...]
        w_all[t, HD:PADW, :] = jnp.zeros((PADW - HD, D), BF)
    gw1.start_z()
    gw2.start_z()
    for w_in, w_all in ((wqkv1, wc1), (wqkv2, wc2)):
        w_all[...] = jnp.concatenate([w_in[j].astype(F32) for j in range(3)], axis=0).astype(BF)
    lanes = lax.broadcasted_iota(jnp.int32, (ROWS, 128), 1)
    vb[...] = jnp.where(lanes == HD, 1.0, 0.0).astype(BF)
    xp[...] = jnp.zeros((BLK, N * PADW), F32)

    @pl.loop(1, N)
    def _(i):
        k = lax.rem(t + i, N)
        remote(tok.at[rows_of(0)], tokr.at[k], tr_s.at[0], tr_r.at[k], (s, k)).wait_recv()

    def side_by_side(blocks):
        for k in range(N):
            xb[:, k * HD:(k + 1) * HD] = blocks[k].astype(F32)

    side_by_side(tokr)
    ga1 = Gather(g1, g1_s, g1_r, p, 2, 3)
    g1[rows_of(t), :] = modulated(xb[...], mod[0:1, :], mod[1:2, :])
    ga1.start()
    pl.semaphore_wait(known_x, 3)
    for dev in z_peers:
        tell(known_z, dev)
    ga1.forward()
    gw1.start_y()
    ga1.relay()
    pl.semaphore_wait(known_z, 3)

    def far_copy(src, dst, ss, rs, r):
        return remote(
            src.at[rows_of(r)], dst.at[t], ss.at[r], rs.at[t], (r, jnp.bitwise_xor(s, r))
        )

    def far_start(src, dst, ss, rs, r):
        own = jnp.logical_and(origin, r == s)

        @pl.when(jnp.logical_not(own))
        def _():
            far_copy(src, dst, ss, rs, r).start()

        @pl.when(own)
        def _():
            dst[t] = src[rows_of(s), :]

    def far_wait_recv(src, dst, ss, rs):
        @pl.loop(0, N)
        def _(i):
            k = lax.rem(t + i, N)

            @pl.when(jnp.logical_not(jnp.logical_and(origin, i == 0)))
            def _():
                remote(
                    src.at[rows_of(0)], dst.at[k], ss.at[0], rs.at[k], p.partner()
                ).wait_recv()

    def far_wait_send(src, dst, ss, rs):
        @pl.loop(0, N)
        def _(r):
            @pl.when(jnp.logical_not(jnp.logical_and(origin, r == s)))
            def _():
                far_copy(src, dst, ss, rs, r).wait_send()

    @pl.loop(0, N)
    def _(i):
        far_start(tok, tokf, tf_s, tf_r, lax.rem(s + i, N))

    ga1.complete()

    @pl.loop(0, 3)
    def _(i):
        rows = pl.ds(pl.multiple_of(i * 256, 256), 256)
        r = dot_nt(g1[rows, :], wc1[...])
        qb[rows, :] = r[:, 0:HD].astype(BF)
        kb[rows, :] = r[:, HD:2 * HD].astype(BF)
        vb[rows, 0:HD] = r[:, 2 * HD:3 * HD].astype(BF)

    @pl.loop(0, 4)
    def _(i):
        part = lax.rem(i + p.zh, 4)
        rows = pl.ds(pl.multiple_of(part * 192, 192), 192)
        scores = dot_nt(qb[rows, :], kb[...])
        top = jnp.max(scores, axis=1, keepdims=True)
        raised = jnp.exp((scores - top) * SCALE).astype(BF)
        mixed = jnp.dot(raised, vb[...], preferred_element_type=F32)
        o1b[rows, :] = (mixed[:, 0:HD] / mixed[:, HD:HD + 1]).astype(BF)
        for j in range(4):
            far_start(o1b, o1f, o1_s, o1_r, part * 4 + lax.rem(p.x + j, 4))

    gw2.start_y()
    gw1.forward()
    far_wait_recv(tok, tokf, tf_s, tf_r)
    side_by_side(tokf)
    gw1.relay()
    far_wait_recv(o1b, o1f, o1_s, o1_r)
    gw1.complete()

    def project(blocks, weights):
        for k in range(N):
            xp[:, k * PADW:k * PADW + HD] = blocks[k].astype(F32)
        return jnp.dot(
            xp[...].astype(BF), weights[...].reshape(N * PADW, D), preferred_element_type=F32
        )

    x1 = (xb[...] + mod[2:3, :] * project(o1f, wo1)).astype(BF).astype(F32)
    xb[...] = x1
    ga2 = Gather(g2, g2_s, g2_r, p, 2, 3)
    g2[rows_of(t), :] = modulated(x1, mod[3:4, :], mod[4:5, :])
    ga2.start()
    ga2.forward()
    gw2.forward()
    ga2.relay()

    mlp_copies = Copies(wm_s)
    for j, (w_in, w_all) in enumerate(((wmi, wia), (wmo, woa))):
        for h, (low, size, device) in enumerate(((0, SHARE, p.z_inner()), (SHARE, FFL - SHARE, p.z_outer()))):
            mlp_copies.push(
                w_in.at[pl.ds(low, size)], w_all.at[1, pl.ds(low, size)], wm_r.at[j, h], device
            )

    ga2.complete()

    @pl.loop(0, 3)
    def _(i):
        rows = pl.ds(pl.multiple_of(i * 256, 256), 256)
        qkvb[rows, :] = dot_nt(g2[rows, :], wc2[...]).astype(BF)

    same = lax.rem(lax.broadcasted_iota(jnp.int32, (256, 256), 0), 16) == lax.rem(
        lax.broadcasted_iota(jnp.int32, (256, 256), 1), 16
    )
    for grp in range(3):
        part = jnp.concatenate(
            [qkvb[f * BLK + grp * 16:f * BLK + grp * 16 + 16, :] for f in range(N)], axis=0
        )
        q, k, v = part[:, 0:HD], part[:, HD:2 * HD], part[:, 2 * HD:3 * HD]
        scores = jnp.where(same, dot_nt(q, k), -1e30)
        top = jnp.max(scores, axis=1, keepdims=True)
        raised = jnp.where(same, jnp.exp((scores - top) * SCALE), 0.0)
        weights = (raised / jnp.sum(raised, axis=1, keepdims=True)).astype(BF)
        mixed = jnp.dot(weights, v, preferred_element_type=F32).astype(BF)
        for f in range(N):
            o2b[f * BLK + grp * 16:f * BLK + grp * 16 + 16, :] = mixed[f * 16:f * 16 + 16, :]

    def o2_copy(i):
        peer = lax.rem(t + i, N)
        return remote(o2b.at[rows_of(peer)], o2r.at[t], o2_s.at[i], o2_r.at[t], (s, peer))

    @pl.loop(1, N)
    def _(i):
        o2_copy(i).start()

    o2r[t] = o2b[rows_of(t), :]
    gw2.relay()

    @pl.loop(1, N)
    def _(i):
        k = lax.rem(t + i, N)
        remote(o2b.at[rows_of(0)], o2r.at[k], o2_s.at[0], o2_r.at[k], (s, k)).wait_recv()

    gw2.complete()
    x2 = (xb[...] + mod[5:6, :] * project(o2r, wo2)).astype(BF).astype(F32)
    xb[...] = x2
    ga3 = Gather(g3, g3_s, g3_r, p, 1, 1)
    g3[rows_of(lax.rem(t, 8)), :] = modulated(x2, mod[6:7, :], mod[7:8, :])
    ga3.start()
    for copy in local:
        copy.wait()
    for j, w_all in enumerate((wia, woa)):
        for h, (low, size) in enumerate(((0, SHARE), (SHARE, FFL - SHARE))):
            ref = w_all.at[1, pl.ds(low, size)]
            remote(ref, ref, wm_s.at[0], wm_r.at[j, h], p.partner()).wait_recv()
    ga3.relay()
    ga3.complete()

    def mlp(cc):
        rows = jnp.concatenate([g3[rows_of(yy * 2 + cc), :] for yy in range(4)], axis=0)
        total = None
        for h in range(2):
            hidden = jax.nn.gelu(dot_nt(rows, wia[h]), approximate=True).astype(BF)
            term = jnp.dot(hidden, woa[h], preferred_element_type=F32)
            total = term if total is None else total + term
        return total

    def ra_copy(j):
        return remote(rs_send.at[j], rs_a.at[j], ra_s.at[j], ra_r.at[j], p.partner())

    r = mlp(1 - p.c)
    for yy in range(4):
        rs_send[yy] = r[yy * BLK:(yy + 1) * BLK, :].astype(BF)
        ra_copy(yy).start()
    r = mlp(p.c)
    for yy in range(4):
        own_sum[yy] = r[yy * BLK:(yy + 1) * BLK, :]

    def chip_sum(yy):
        ra_copy(yy).wait_recv()
        return own_sum[yy] + rs_a[yy].astype(F32)

    def ry_copy(j, yy):
        return remote(mid.at[j], rs_y.at[j], ry_s.at[j], ry_r.at[j], p.dev(p.z, yy, p.c))

    ring = (p.far, p.up, p.down)
    for j, yy in enumerate(ring):
        mid[j] = chip_sum(yy).astype(BF)
        ry_copy(j, yy).start()
    total = chip_sum(p.y)
    for j, yy in enumerate(ring):
        ry_copy(j, yy).wait_recv()
        total = total + rs_y[j].astype(F32)
    result = (xb[...] + mod[8:9, :] * total).astype(BF)
    for k in range(N):
        res_s[k] = result[:, k * HD:(k + 1) * HD]

    def res_copy(i):
        k = lax.rem(t + i, N)
        return remote(res_s.at[k], res_r.at[rows_of(s)], re_s.at[i], re_r.at[s], (frame, k))

    @pl.when(jnp.logical_not(origin))
    def _():
        res_copy(0).start()

    @pl.when(origin)
    def _():
        res_r[rows_of(s), :] = res_s[t]

    @pl.loop(1, N)
    def _(i):
        res_copy(i).start()

    @pl.loop(1, N)
    def _(i):
        tok_copy(i).wait_send()
        o2_copy(i).wait_send()

    far_wait_send(tok, tokf, tf_s, tf_r)
    far_wait_send(o1b, o1f, o1_s, o1_r)
    for g in (ga1, ga2, ga3, gw1, gw2):
        g.copies.finish()
    mlp_copies.finish()
    for yy in range(4):
        ra_copy(yy).wait_send()
    for j, yy in enumerate(ring):
        ry_copy(j, yy).wait_send()

    @pl.when(jnp.logical_not(origin))
    def _():
        res_copy(0).wait_send()
        remote(res_s.at[0], res_r.at[rows_of(s)], re_s.at[0], re_r.at[s], p.partner()).wait_recv()

    @pl.loop(1, N)
    def _(i):
        res_copy(i).wait_send()
        k = lax.rem(s + i, N)
        remote(res_s.at[0], res_r.at[rows_of(k)], re_s.at[0], re_r.at[k], p.partner()).wait_recv()

    out_t[...] = jnp.transpose(res_r[...].astype(F32)).astype(BF)


def per_device(tokens, modulation, spatial_qkv, spatial_out, temporal_qkv, temporal_out, mlp_in, mlp_out):
    vm = pltpu.VMEM
    dma = pltpu.SemaphoreType.DMA
    regular = pltpu.SemaphoreType.REGULAR
    scratch = [
        vm((ROWS, HD), BF),
        vm((N, BLK, HD), BF),
        vm((N, BLK, HD), BF),
        vm((ROWS, D), BF),
        vm((ROWS, D), BF),
        vm((ROWS // 2, D), BF),
        vm((N, PADW, D), BF),
        vm((N, PADW, D), BF),
        vm((3 * HD, D), BF),
        vm((3 * HD, D), BF),
        vm((2, FFL, D), BF),
        vm((2, FFL, D), BF),
        vm((ROWS, HD), BF),
        vm((ROWS, HD), BF),
        vm((ROWS, 128), BF),
        vm((ROWS, HD), BF),
        vm((N, BLK, HD), BF),
        vm((ROWS, 3 * HD), BF),
        vm((ROWS, HD), BF),
        vm((N, BLK, HD), BF),
        vm((BLK, D), F32),
        vm((BLK, N * PADW), F32),
        vm((4, BLK, D), BF),
        vm((4, BLK, D), BF),
        vm((4, BLK, D), F32),
        vm((3, BLK, D), BF),
        vm((3, BLK, D), BF),
        vm((N, BLK, HD), BF),
        vm((ROWS, HD), BF),
        regular,
        regular,
    ]
    scratch += [dma((N,))] * 10
    scratch += [dma((64,)), dma((N, 3))] * 3
    scratch += [dma((24,)), dma((N, 2))] * 2
    scratch += [dma((4,)), dma((2, 2)), dma((2,))]
    scratch += [dma((4,)), dma((4,)), dma((3,)), dma((3,))]
    return pl.pallas_call(
        kernel,
        out_shape=jax.ShapeDtypeStruct((HD, ROWS), BF),
        in_specs=[pl.BlockSpec(memory_space=pltpu.VMEM)] * 6
        + [pl.BlockSpec(memory_space=pl.ANY)] * 2,
        out_specs=pl.BlockSpec(memory_space=pltpu.VMEM),
        scratch_shapes=scratch,
        compiler_params=pltpu.CompilerParams(
            collective_id=0, has_side_effects=True, vmem_limit_bytes=50 * 1024 * 1024
        ),
        cost_estimate=pl.CostEstimate(
            flops=2_300_000_000, bytes_accessed=4_000_000, transcendentals=1_000_000
        ),
    )(
        tokens.T,
        modulation,
        jnp.swapaxes(spatial_qkv, 1, 2),
        spatial_out,
        jnp.swapaxes(temporal_qkv, 1, 2),
        temporal_out,
        mlp_in.T,
        mlp_out,
    ).T


def solution(mesh):
    return jax.shard_map(
        per_device,
        mesh=mesh,
        in_specs=(
            P("seq", "tp"),
            P(),
            P(None, None, "tp"),
            P("tp", None),
            P(None, None, "tp"),
            P("tp", None),
            P(None, "tp"),
            P("tp", None),
        ),
        out_specs=P("seq", "tp"),
        check_vma=False,
    )
```

```python
import jax
import jax.numpy as jnp
from jax import lax
from jax.experimental import pallas as pl
from jax.experimental.pallas import tpu as pltpu
from jax.sharding import PartitionSpec as P

HD = 72
D = 1152
N = 16
ROWS = 768
BLK = 48
PK = 32
FFL = 288
PADW = 80
CUT = 48
SHARE = 144
EPS = 1e-06
SCALE = HD ** (-0.5)
BF = jnp.bfloat16
F32 = jnp.float32


def remote(src, dst, send_sem, recv_sem, device):
    return pltpu.make_async_remote_copy(
        src_ref=src,
        dst_ref=dst,
        send_sem=send_sem,
        recv_sem=recv_sem,
        device_id=device,
        device_id_type=pl.DeviceIdType.MESH,
    )


def dot_nt(a, b):
    return lax.dot_general(a, b, (((1,), (1,)), ((), ())), preferred_element_type=F32)


def modulated(rows, shift, scale):
    average = jnp.mean(rows, axis=-1, keepdims=True)
    centred = rows - average
    variance = jnp.mean(centred * centred, axis=-1, keepdims=True)
    return (centred * lax.rsqrt(variance + EPS) * (1.0 + scale) + shift).astype(BF)


def pack(dst, i, block):
    dst[i, :, 0:HD] = block[0:PK, :]
    dst[i, 0:16, HD:128] = block[PK:BLK, 0:128 - HD]
    dst[i, 16:PK, HD:2 * HD - 56] = block[PK:BLK, 56:HD]


def unpack(dst, row, low, src, i):
    block = src[i].astype(F32)
    dst[row:row + PK, low:low + HD] = block[:, 0:HD]
    dst[row + PK:row + BLK, low:low + 56] = block[0:16, HD:128]
    dst[row + PK:row + BLK, low + 56:low + HD] = block[16:PK, HD:2 * HD - 56]


class Copies:
    def __init__(self, send):
        self.send = send
        self.started = []

    def push(self, src, dst, recv, device):
        copy = remote(src, dst, self.send.at[len(self.started)], recv, device)
        copy.start()
        self.started.append(copy)

    def finish(self):
        for copy in self.started:
            copy.wait_send()


class Place:
    def __init__(self):
        self.s = lax.axis_index("seq")
        self.t = lax.axis_index("tp")
        self.z = lax.div(self.t, 8)
        self.y = lax.rem(lax.div(self.t, 2), 4)
        self.c = lax.rem(self.t, 2)
        self.zh = lax.div(self.s, 4)
        self.x = lax.rem(self.s, 4)
        self.up = lax.rem(self.y + 1, 4)
        self.down = lax.rem(self.y + 3, 4)
        self.far = lax.rem(self.y + 2, 4)

    def at(self, z, y, c):
        return z * 8 + y * 2 + c

    def dev(self, z, y, c):
        return (self.s, self.at(z, y, c))

    def partner(self):
        return self.dev(self.z, self.y, 1 - self.c)

    def z_inner(self):
        return self.dev(1 - self.z, self.y, self.c)

    def z_outer(self):
        zh = lax.rem(self.zh + jnp.where(self.z == 1, 1, 3), 4)
        return (zh * 4 + self.x, self.at(1 - self.z, self.y, self.c))


class Gather:
    def __init__(self, buf, send, recv, at, planes, chunks):
        self.buf, self.recv, self.p, self.planes, self.chunks = buf, recv, at, planes, chunks
        self.rows = BLK // chunks
        self.copies = Copies(send)

    def slot(self, o, k):
        if self.planes == 1:
            o = lax.rem(o, 8)
        return self.buf.at[pl.ds(pl.multiple_of(o * BLK + k * self.rows, self.rows), self.rows)]

    def sem(self, o, k):
        return self.recv.at[o, k]

    def push(self, o, k, device):
        ref = self.slot(o, k)
        self.copies.push(ref, ref, self.sem(o, k), device)

    def arrive(self, o, k):
        ref = self.slot(o, k)
        remote(ref, ref, self.copies.send.at[0], self.sem(o, k), self.p.partner()).wait_recv()

    def start(self):
        p = self.p
        for k in range(self.chunks):
            if self.planes == 2:
                self.push(p.t, k, p.z_inner())
            for yy in (p.up, p.down, p.far):
                self.push(p.t, k, p.dev(p.z, yy, p.c))
        for k in range(self.chunks):
            self.push(p.t, k, p.partner())

    def forward(self):
        p = self.p
        if self.planes == 1:
            return
        for k in range(self.chunks):
            o = p.at(1 - p.z, p.y, p.c)
            self.arrive(o, k)
            for yy in (p.up, p.down):
                self.push(o, k, p.dev(p.z, yy, p.c))
            self.push(o, k, p.partner())
        for k in range(self.chunks):
            o = p.at(p.z, p.far, p.c)
            self.arrive(o, k)
            self.push(o, k, p.z_inner())
            self.push(o, k, p.partner())

    def relay(self):
        p = self.p
        near = (p.up, p.down) if self.planes == 2 else (p.up, p.down, p.far)
        for k in range(self.chunks):
            for yy in near:
                o = p.at(p.z, yy, p.c)
                self.arrive(o, k)
                self.push(o, k, p.partner())
        if self.planes == 2:
            for k in range(self.chunks):
                for yy in (p.up, p.down, p.far):
                    o = p.at(1 - p.z, yy, p.c)
                    self.arrive(o, k)
                    self.push(o, k, p.partner())

    def complete(self):
        p = self.p
        for zz in (p.z, 1 - p.z)[: self.planes]:
            for yy in (p.y, p.up, p.down, p.far):
                for k in range(self.chunks):
                    self.arrive(p.at(zz, yy, 1 - p.c), k)


class WeightGather:
    def __init__(self, buf, send, recv, at):
        self.buf, self.recv, self.p = buf, recv, at
        self.copies = Copies(send)

    def part(self, o, h):
        return self.buf.at[o, pl.ds(0, CUT)] if h == 0 else self.buf.at[o, pl.ds(CUT, PADW - CUT)]

    def halves(self, o):
        p = self.p
        for h, device in ((0, p.z_inner()), (1, p.z_outer())):
            ref = self.part(o, h)
            self.copies.push(ref, ref, self.recv.at[o, h], device)

    def whole(self, o, device):
        ref = self.buf.at[o]
        self.copies.push(ref, ref, self.recv.at[o, 0], device)

    def arrive(self, o):
        ref = self.buf.at[o]
        remote(ref, ref, self.copies.send.at[0], self.recv.at[o, 0], self.p.partner()).wait_recv()

    def arrive_parts(self, o):
        for h in range(2):
            ref = self.part(o, h)
            remote(
                ref, ref, self.copies.send.at[0], self.recv.at[o, h], self.p.partner()
            ).wait_recv()

    def start_z(self):
        self.halves(self.p.t)

    def start_y(self, h):
        p = self.p
        ref = self.part(p.t, h)
        for yy in (p.far, p.up, p.down):
            self.copies.push(ref, ref, self.recv.at[p.t, h], p.dev(p.z, yy, p.c))
        if h == 0:
            self.whole(p.t, p.partner())

    def forward(self):
        p = self.p
        for yy in (p.up, p.down, p.far):
            o = p.at(p.z, yy, p.c)
            self.arrive_parts(o)
            self.halves(o)
            self.whole(o, p.partner())

    def relay(self):
        p = self.p
        for yy in (p.y, p.up, p.down, p.far):
            o = p.at(1 - p.z, yy, p.c)
            self.arrive_parts(o)
            self.whole(o, p.partner())

    def complete(self):
        p = self.p
        for zz in (p.z, 1 - p.z):
            for yy in (p.y, p.up, p.down, p.far):
                self.arrive(p.at(zz, yy, 1 - p.c))


def kernel(
    tok_h, mod_h, wqkv1_h, wout1_h, wqkv2_h, wout2_h, wmi_h, wmo_h, out_t,
    tok_t, mod, wqkv1, wout1, wqkv2, wout2, tok, tokr, x0b, x0f, g1, g2, g3, wo1, wo2, wc1, wc2, wia, woa,
    qb, kb, vb, o1b, o1f, qkvb, o2b, o2p, o2r, xb, xp, rows_f,
    rs_send, rs_a, own_sum, mid, rs_y, res_s, res_r,
    known_x, known_z,
    tr_s, tr_r, tf_s, tf_r, o1_s, o1_r, o2_s, o2_r, re_s, re_r,
    g1_s, g1_r, g2_s, g2_r, g3_s, g3_r, w1_s, w1_r, w2_s, w2_r, wm_s, wm_r, wl_s,
    ra_s, ra_r, ry_s, ry_r,
):
    p = Place()
    s, t = p.s, p.t
    frame = jnp.bitwise_xor(s, t)
    origin = t == 0

    def rows_of(i):
        return pl.ds(pl.multiple_of(i * BLK, BLK), BLK)

    def tell(sem, dev):
        pl.semaphore_signal(sem, inc=1, device_id=dev, device_id_type=pl.DeviceIdType.MESH)

    inward = [
        pltpu.make_async_copy(src, dst, wl_s.at[j])
        for j, (src, dst) in enumerate(
            (
                (tok_h, tok_t),
                (mod_h, mod),
                (wout1_h, wout1),
                (wout2_h, wout2),
                (wqkv1_h, wqkv1),
                (wqkv2_h, wqkv2),
                (wmi_h, wia.at[0]),
                (wmo_h, woa.at[0]),
            )
        )
    ]
    for copy in inward:
        copy.start()

    barrier = pltpu.get_barrier_semaphore()
    x_peers = [(p.zh * 4 + lax.rem(p.x + j, 4), t) for j in (1, 2, 3)]
    z_peers = [(lax.rem(p.zh + j, 4) * 4 + p.x, t) for j in (1, 2, 3)]

    for dev in x_peers + z_peers + [p.z_outer()]:
        tell(barrier, dev)

    @pl.loop(1, N)
    def _(i):
        tell(barrier, (s, lax.rem(t + i, N)))

    inward[0].wait()
    rows = jnp.transpose(tok_t[...].astype(F32)).astype(BF)
    for k in range(N):
        pack(tok, k, rows[k * BLK:(k + 1) * BLK, :])
    pl.semaphore_wait(barrier, 22)

    def tok_copy(i):
        peer = lax.rem(t + i, N)
        return remote(tok.at[peer], tokr.at[t], tr_s.at[i], tr_r.at[t], (s, peer))

    @pl.loop(1, N)
    def _(i):
        tok_copy(i).start()

    tokr[t] = tok[t]
    for dev in x_peers:
        tell(known_x, dev)

    for copy in inward[1:6]:
        copy.wait()
    gw1 = WeightGather(wo1, w1_s, w1_r, p)
    gw2 = WeightGather(wo2, w2_s, w2_r, p)
    for w_in, w_all in ((wout1, wo1), (wout2, wo2)):
        w_all[t, 0:HD, :] = w_in[...]
        w_all[t, HD:PADW, :] = jnp.zeros((PADW - HD, D), BF)
    gw1.start_z()
    gw1.start_y(1)
    gw2.start_z()
    for w_in, w_all in ((wqkv1, wc1), (wqkv2, wc2)):
        w_all[...] = jnp.concatenate([w_in[j].astype(F32) for j in range(3)], axis=0).astype(BF)
    lanes = lax.broadcasted_iota(jnp.int32, (ROWS, 128), 1)
    vb[...] = jnp.where(lanes == HD, 1.0, 0.0).astype(BF)
    xp[...] = jnp.zeros((BLK, N * PADW), F32)

    @pl.loop(1, N)
    def _(i):
        k = lax.rem(t + i, N)
        remote(tok.at[0], tokr.at[k], tr_s.at[0], tr_r.at[k], (s, k)).wait_recv()

    def side_by_side(blocks):
        for k in range(N):
            unpack(xb, 0, k * HD, blocks, k)

    side_by_side(tokr)
    x0b[...] = xb[...].astype(BF)
    ga1 = Gather(g1, g1_s, g1_r, p, 2, 3)
    g1[rows_of(t), :] = modulated(xb[...], mod[0:1, :], mod[1:2, :])
    ga1.start()
    pl.semaphore_wait(known_x, 3)
    for dev in z_peers:
        tell(known_z, dev)
    ga1.forward()
    gw1.start_y(0)
    ga1.relay()
    pl.semaphore_wait(known_z, 3)

    def far_copy(src, dst, ss, rs, r):
        return remote(
            src.at[r], dst.at[t], ss.at[r], rs.at[t], (r, jnp.bitwise_xor(s, r))
        )

    def far_start(src, dst, ss, rs, r):
        own = jnp.logical_and(origin, r == s)

        @pl.when(jnp.logical_not(own))
        def _():
            far_copy(src, dst, ss, rs, r).start()

        @pl.when(own)
        def _():
            dst[t] = src[s]

    def far_wait_recv(src, dst, ss, rs):
        @pl.loop(0, N)
        def _(i):
            k = lax.rem(t + i, N)

            @pl.when(jnp.logical_not(jnp.logical_and(origin, i == 0)))
            def _():
                remote(
                    src.at[0], dst.at[k], ss.at[0], rs.at[k], p.partner()
                ).wait_recv()

    def far_wait_send(src, dst, ss, rs):
        @pl.loop(0, N)
        def _(r):
            @pl.when(jnp.logical_not(jnp.logical_and(origin, r == s)))
            def _():
                far_copy(src, dst, ss, rs, r).wait_send()

    corner = jnp.logical_and(s == 0, t == 0)
    row_copy = remote(x0b, x0f, tf_s, tf_r, (t, frame))

    @pl.when(jnp.logical_not(corner))
    def _():
        row_copy.start()

    @pl.when(corner)
    def _():
        x0f[...] = x0b[...]

    ga1.complete()

    @pl.loop(0, 3)
    def _(i):
        rows = pl.ds(pl.multiple_of(i * 256, 256), 256)
        r = dot_nt(g1[rows, :], wc1[...])
        qb[rows, :] = r[:, 0:HD].astype(BF)
        kb[rows, :] = r[:, HD:2 * HD].astype(BF)
        vb[rows, 0:HD] = r[:, 2 * HD:3 * HD].astype(BF)

    @pl.loop(0, 4)
    def _(i):
        part = lax.rem(i + p.zh, 4)
        rows = pl.ds(pl.multiple_of(part * 192, 192), 192)
        scores = dot_nt(qb[rows, :], kb[...])
        top = jnp.max(scores, axis=1, keepdims=True)
        raised = jnp.exp((scores - top) * SCALE).astype(BF)
        mixed = jnp.dot(raised, vb[...], preferred_element_type=F32)
        mixed = (mixed[:, 0:HD] / mixed[:, HD:HD + 1]).astype(BF)
        for j in range(4):
            pack(o1b, part * 4 + j, mixed[j * BLK:(j + 1) * BLK, :])
        for j in range(4):
            far_start(o1b, o1f, o1_s, o1_r, part * 4 + lax.rem(p.x + j, 4))

    gw2.start_y(1)
    gw2.start_y(0)
    gw1.forward()
    @pl.when(jnp.logical_not(corner))
    def _():
        row_copy.wait_recv()

    gw1.relay()
    far_wait_recv(o1b, o1f, o1_s, o1_r)
    gw1.complete()

    def project(blocks, weights):
        for k in range(N):
            unpack(xp, 0, k * PADW, blocks, k)
        return jnp.dot(
            xp[...].astype(BF), weights[...].reshape(N * PADW, D), preferred_element_type=F32
        )

    x1 = (x0f[...].astype(F32) + mod[2:3, :] * project(o1f, wo1)).astype(BF).astype(F32)
    xb[...] = x1
    ga2 = Gather(g2, g2_s, g2_r, p, 2, 3)
    g2[rows_of(t), :] = modulated(x1, mod[3:4, :], mod[4:5, :])
    ga2.start()
    ga2.forward()
    gw2.forward()
    ga2.relay()

    ga2.complete()

    @pl.loop(0, 3)
    def _(i):
        rows = pl.ds(pl.multiple_of(i * 256, 256), 256)
        qkvb[rows, :] = dot_nt(g2[rows, :], wc2[...]).astype(BF)

    same = lax.rem(lax.broadcasted_iota(jnp.int32, (256, 256), 0), 16) == lax.rem(
        lax.broadcasted_iota(jnp.int32, (256, 256), 1), 16
    )
    for grp in range(3):
        part = jnp.concatenate(
            [qkvb[f * BLK + grp * 16:f * BLK + grp * 16 + 16, :] for f in range(N)], axis=0
        )
        q, k, v = part[:, 0:HD], part[:, HD:2 * HD], part[:, 2 * HD:3 * HD]
        scores = jnp.where(same, dot_nt(q, k), -1e30)
        top = jnp.max(scores, axis=1, keepdims=True)
        raised = jnp.where(same, jnp.exp((scores - top) * SCALE), 0.0)
        weights = (raised / jnp.sum(raised, axis=1, keepdims=True)).astype(BF)
        mixed = jnp.dot(weights, v, preferred_element_type=F32).astype(BF)
        for f in range(N):
            o2b[f * BLK + grp * 16:f * BLK + grp * 16 + 16, :] = mixed[f * 16:f * 16 + 16, :]

    for f in range(N):
        pack(o2p, f, o2b[f * BLK:(f + 1) * BLK, :])

    def o2_copy(i):
        peer = lax.rem(t + i, N)
        return remote(o2p.at[peer], o2r.at[t], o2_s.at[i], o2_r.at[t], (s, peer))

    @pl.loop(1, N)
    def _(i):
        o2_copy(i).start()

    o2r[t] = o2p[t]
    for copy in inward[6:]:
        copy.wait()
    mlp_copies = Copies(wm_s)
    for j, w_all in enumerate((wia, woa)):
        for h, (low, size, device) in enumerate(((0, SHARE, p.z_inner()), (SHARE, FFL - SHARE, p.z_outer()))):
            mlp_copies.push(
                w_all.at[0, pl.ds(low, size)], w_all.at[1, pl.ds(low, size)], wm_r.at[j, h], device
            )

    gw2.relay()

    @pl.loop(1, N)
    def _(i):
        k = lax.rem(t + i, N)
        remote(o2p.at[0], o2r.at[k], o2_s.at[0], o2_r.at[k], (s, k)).wait_recv()

    gw2.complete()
    x2 = (xb[...] + mod[5:6, :] * project(o2r, wo2)).astype(BF).astype(F32)
    xb[...] = x2
    ga3 = Gather(g3, g3_s, g3_r, p, 1, 1)
    g3[rows_of(lax.rem(t, 8)), :] = modulated(x2, mod[6:7, :], mod[7:8, :])
    ga3.start()
    for j, w_all in enumerate((wia, woa)):
        for h, (low, size) in enumerate(((0, SHARE), (SHARE, FFL - SHARE))):
            ref = w_all.at[1, pl.ds(low, size)]
            remote(ref, ref, wm_s.at[0], wm_r.at[j, h], p.partner()).wait_recv()
    ga3.relay()
    ga3.complete()

    def mlp(cc):
        rows = jnp.concatenate([g3[rows_of(yy * 2 + cc), :] for yy in range(4)], axis=0)
        total = None
        for h in range(2):
            hidden = jax.nn.gelu(dot_nt(rows, wia[h]), approximate=True).astype(BF)
            term = jnp.dot(hidden, woa[h], preferred_element_type=F32)
            total = term if total is None else total + term
        return total

    def ra_copy(j):
        return remote(rs_send.at[j], rs_a.at[j], ra_s.at[j], ra_r.at[j], p.partner())

    r = mlp(1 - p.c)
    for yy in range(4):
        rs_send[yy] = r[yy * BLK:(yy + 1) * BLK, :].astype(BF)
        ra_copy(yy).start()
    r = mlp(p.c)
    for yy in range(4):
        own_sum[yy] = r[yy * BLK:(yy + 1) * BLK, :]

    def chip_sum(yy):
        ra_copy(yy).wait_recv()
        return own_sum[yy] + rs_a[yy].astype(F32)

    def ry_copy(j, yy):
        return remote(mid.at[j], rs_y.at[j], ry_s.at[j], ry_r.at[j], p.dev(p.z, yy, p.c))

    ring = (p.far, p.up, p.down)
    for j, yy in enumerate(ring):
        mid[j] = chip_sum(yy).astype(BF)
        ry_copy(j, yy).start()
    total = chip_sum(p.y)
    for j, yy in enumerate(ring):
        ry_copy(j, yy).wait_recv()
        total = total + rs_y[j].astype(F32)
    result = (xb[...] + mod[8:9, :] * total).astype(BF)
    for k in range(N):
        pack(res_s, k, result[:, k * HD:(k + 1) * HD])

    def res_copy(i):
        k = lax.rem(t + i, N)
        return remote(res_s.at[k], res_r.at[s], re_s.at[i], re_r.at[s], (frame, k))

    @pl.when(jnp.logical_not(origin))
    def _():
        res_copy(0).start()

    @pl.when(origin)
    def _():
        res_r[s] = res_s[t]

    @pl.loop(1, N)
    def _(i):
        res_copy(i).start()

    @pl.loop(1, N)
    def _(i):
        tok_copy(i).wait_send()
        o2_copy(i).wait_send()

    @pl.when(jnp.logical_not(corner))
    def _():
        row_copy.wait_send()

    far_wait_send(o1b, o1f, o1_s, o1_r)
    for g in (ga1, ga2, ga3, gw1, gw2):
        g.copies.finish()
    mlp_copies.finish()
    for yy in range(4):
        ra_copy(yy).wait_send()
    for j, yy in enumerate(ring):
        ry_copy(j, yy).wait_send()

    @pl.when(jnp.logical_not(origin))
    def _():
        res_copy(0).wait_send()
        remote(res_s.at[0], res_r.at[s], re_s.at[0], re_r.at[s], p.partner()).wait_recv()

    @pl.loop(1, N)
    def _(i):
        res_copy(i).wait_send()
        k = lax.rem(s + i, N)
        remote(res_s.at[0], res_r.at[k], re_s.at[0], re_r.at[k], p.partner()).wait_recv()

    for k in range(N):
        unpack(rows_f, k * BLK, 0, res_r, k)
    out_t[...] = jnp.transpose(rows_f[...]).astype(BF)


def per_device(tokens, modulation, spatial_qkv, spatial_out, temporal_qkv, temporal_out, mlp_in, mlp_out):
    vm = pltpu.VMEM
    dma = pltpu.SemaphoreType.DMA
    regular = pltpu.SemaphoreType.REGULAR
    scratch = [
        vm((HD, ROWS), BF),
        vm((9, D), F32),
        vm((3, HD, D), BF),
        vm((HD, D), BF),
        vm((3, HD, D), BF),
        vm((HD, D), BF),
        vm((N, PK, 128), BF),
        vm((N, PK, 128), BF),
        vm((BLK, D), BF),
        vm((BLK, D), BF),
        vm((ROWS, D), BF),
        vm((ROWS, D), BF),
        vm((ROWS // 2, D), BF),
        vm((N, PADW, D), BF),
        vm((N, PADW, D), BF),
        vm((3 * HD, D), BF),
        vm((3 * HD, D), BF),
        vm((2, FFL, D), BF),
        vm((2, FFL, D), BF),
        vm((ROWS, HD), BF),
        vm((ROWS, HD), BF),
        vm((ROWS, 128), BF),
        vm((N, PK, 128), BF),
        vm((N, PK, 128), BF),
        vm((ROWS, 3 * HD), BF),
        vm((ROWS, HD), BF),
        vm((N, PK, 128), BF),
        vm((N, PK, 128), BF),
        vm((BLK, D), F32),
        vm((BLK, N * PADW), F32),
        vm((ROWS, HD), F32),
        vm((4, BLK, D), BF),
        vm((4, BLK, D), BF),
        vm((4, BLK, D), F32),
        vm((3, BLK, D), BF),
        vm((3, BLK, D), BF),
        vm((N, PK, 128), BF),
        vm((N, PK, 128), BF),
        regular,
        regular,
    ]
    scratch += [dma((N,))] * 2 + [dma, dma] + [dma((N,))] * 6
    scratch += [dma((64,)), dma((N, 3))] * 3
    scratch += [dma((24,)), dma((N, 2))] * 2
    scratch += [dma((4,)), dma((2, 2)), dma((8,))]
    scratch += [dma((4,)), dma((4,)), dma((3,)), dma((3,))]
    return pl.pallas_call(
        kernel,
        out_shape=jax.ShapeDtypeStruct((HD, ROWS), BF),
        in_specs=[pl.BlockSpec(memory_space=pltpu.HBM)] * 8,
        out_specs=pl.BlockSpec(memory_space=pltpu.VMEM),
        scratch_shapes=scratch,
        compiler_params=pltpu.CompilerParams(
            collective_id=0, has_side_effects=True, vmem_limit_bytes=60 * 1024 * 1024
        ),
        cost_estimate=pl.CostEstimate(
            flops=2_300_000_000, bytes_accessed=4_000_000, transcendentals=1_000_000
        ),
    )(
        tokens.T,
        modulation,
        jnp.swapaxes(spatial_qkv, 1, 2),
        spatial_out,
        jnp.swapaxes(temporal_qkv, 1, 2),
        temporal_out,
        mlp_in.T,
        mlp_out,
    ).T


def solution(mesh):
    return jax.shard_map(
        per_device,
        mesh=mesh,
        in_specs=(
            P("seq", "tp"),
            P(),
            P(None, None, "tp"),
            P("tp", None),
            P(None, None, "tp"),
            P("tp", None),
            P(None, "tp"),
            P("tp", None),
        ),
        out_specs=P("seq", "tp"),
        check_vma=False,
    )
```

```python
import jax
import jax.numpy as jnp
from jax import lax
from jax.experimental import pallas as pl
from jax.experimental.pallas import tpu as pltpu
from jax.sharding import PartitionSpec as P

HD = 72
D = 1152
N = 16
ROWS = 768
BLK = 48
PK = 32
FFL = 288
PADW = 80
CUT = 48
MLP_PARTS = ((0, 144, True), (144, 64, True), (208, 80, False))
EPS = 1e-06
SCALE = HD ** (-0.5)
BF = jnp.bfloat16
F32 = jnp.float32


def remote(src, dst, send_sem, recv_sem, device):
    return pltpu.make_async_remote_copy(
        src_ref=src,
        dst_ref=dst,
        send_sem=send_sem,
        recv_sem=recv_sem,
        device_id=device,
        device_id_type=pl.DeviceIdType.MESH,
    )


def dot_nt(a, b):
    return lax.dot_general(a, b, (((1,), (1,)), ((), ())), preferred_element_type=F32)


def modulated(rows, shift, scale):
    average = jnp.mean(rows, axis=-1, keepdims=True)
    centred = rows - average
    variance = jnp.mean(centred * centred, axis=-1, keepdims=True)
    return (centred * lax.rsqrt(variance + EPS) * (1.0 + scale) + shift).astype(BF)


def pack(dst, i, block):
    dst[i, :, 0:HD] = block[0:PK, :]
    dst[i, 0:16, HD:128] = block[PK:BLK, 0:128 - HD]
    dst[i, 16:PK, HD:2 * HD - 56] = block[PK:BLK, 56:HD]


def unpack(dst, row, low, src, i):
    block = src[i].astype(F32)
    dst[row:row + PK, low:low + HD] = block[:, 0:HD]
    dst[row + PK:row + BLK, low:low + 56] = block[0:16, HD:128]
    dst[row + PK:row + BLK, low + 56:low + HD] = block[16:PK, HD:2 * HD - 56]


class Copies:
    def __init__(self, send):
        self.send = send
        self.started = []

    def push(self, src, dst, recv, device):
        copy = remote(src, dst, self.send.at[len(self.started)], recv, device)
        copy.start()
        self.started.append(copy)

    def finish(self):
        for copy in self.started:
            copy.wait_send()


class Place:
    def __init__(self):
        self.s = lax.axis_index("seq")
        self.t = lax.axis_index("tp")
        self.z = lax.div(self.t, 8)
        self.y = lax.rem(lax.div(self.t, 2), 4)
        self.c = lax.rem(self.t, 2)
        self.zh = lax.div(self.s, 4)
        self.x = lax.rem(self.s, 4)
        self.up = lax.rem(self.y + 1, 4)
        self.down = lax.rem(self.y + 3, 4)
        self.far = lax.rem(self.y + 2, 4)

    def at(self, z, y, c):
        return z * 8 + y * 2 + c

    def dev(self, z, y, c):
        return (self.s, self.at(z, y, c))

    def partner(self):
        return self.dev(self.z, self.y, 1 - self.c)

    def z_inner(self):
        return self.dev(1 - self.z, self.y, self.c)

    def z_outer(self):
        zh = lax.rem(self.zh + jnp.where(self.z == 1, 1, 3), 4)
        return (zh * 4 + self.x, self.at(1 - self.z, self.y, self.c))


class Gather:
    def __init__(self, buf, send, recv, at, planes, chunks):
        self.buf, self.recv, self.p, self.planes, self.chunks = buf, recv, at, planes, chunks
        self.rows = BLK // chunks
        self.copies = Copies(send)

    def slot(self, o, k):
        if self.planes == 1:
            o = lax.rem(o, 8)
        return self.buf.at[pl.ds(pl.multiple_of(o * BLK + k * self.rows, self.rows), self.rows)]

    def sem(self, o, k):
        return self.recv.at[o, k]

    def push(self, o, k, device):
        ref = self.slot(o, k)
        self.copies.push(ref, ref, self.sem(o, k), device)

    def arrive(self, o, k):
        ref = self.slot(o, k)
        remote(ref, ref, self.copies.send.at[0], self.sem(o, k), self.p.partner()).wait_recv()

    def start(self):
        p = self.p
        for k in range(self.chunks):
            if self.planes == 2:
                self.push(p.t, k, p.z_inner())
            for yy in (p.up, p.down, p.far):
                self.push(p.t, k, p.dev(p.z, yy, p.c))
        for k in range(self.chunks):
            self.push(p.t, k, p.partner())

    def forward(self):
        p = self.p
        if self.planes == 1:
            return
        for k in range(self.chunks):
            o = p.at(1 - p.z, p.y, p.c)
            self.arrive(o, k)
            for yy in (p.up, p.down):
                self.push(o, k, p.dev(p.z, yy, p.c))
            self.push(o, k, p.partner())
        for k in range(self.chunks):
            o = p.at(p.z, p.far, p.c)
            self.arrive(o, k)
            self.push(o, k, p.z_inner())
            self.push(o, k, p.partner())

    def relay(self):
        p = self.p
        near = (p.up, p.down) if self.planes == 2 else (p.up, p.down, p.far)
        for k in range(self.chunks):
            for yy in near:
                o = p.at(p.z, yy, p.c)
                self.arrive(o, k)
                self.push(o, k, p.partner())
        if self.planes == 2:
            for k in range(self.chunks):
                for yy in (p.up, p.down, p.far):
                    o = p.at(1 - p.z, yy, p.c)
                    self.arrive(o, k)
                    self.push(o, k, p.partner())

    def complete(self):
        p = self.p
        for zz in (p.z, 1 - p.z)[: self.planes]:
            for yy in (p.y, p.up, p.down, p.far):
                for k in range(self.chunks):
                    self.arrive(p.at(zz, yy, 1 - p.c), k)


class WeightGather:
    def __init__(self, buf, send, recv, at):
        self.buf, self.recv, self.p = buf, recv, at
        self.copies = Copies(send)

    def part(self, o, h):
        return self.buf.at[o, pl.ds(0, CUT)] if h == 0 else self.buf.at[o, pl.ds(CUT, PADW - CUT)]

    def halves(self, o):
        p = self.p
        for h, device in ((0, p.z_inner()), (1, p.z_outer())):
            ref = self.part(o, h)
            self.copies.push(ref, ref, self.recv.at[o, h], device)

    def whole(self, o, device):
        ref = self.buf.at[o]
        self.copies.push(ref, ref, self.recv.at[o, 0], device)

    def arrive(self, o):
        ref = self.buf.at[o]
        remote(ref, ref, self.copies.send.at[0], self.recv.at[o, 0], self.p.partner()).wait_recv()

    def arrive_parts(self, o):
        for h in range(2):
            ref = self.part(o, h)
            remote(
                ref, ref, self.copies.send.at[0], self.recv.at[o, h], self.p.partner()
            ).wait_recv()

    def start_z(self):
        self.halves(self.p.t)

    def start_y(self, h):
        p = self.p
        ref = self.part(p.t, h)
        for yy in (p.far, p.up, p.down):
            self.copies.push(ref, ref, self.recv.at[p.t, h], p.dev(p.z, yy, p.c))
        if h == 0:
            self.whole(p.t, p.partner())

    def forward(self):
        p = self.p
        for yy in (p.up, p.down, p.far):
            o = p.at(p.z, yy, p.c)
            self.arrive_parts(o)
            self.halves(o)
            self.whole(o, p.partner())

    def relay(self):
        p = self.p
        for yy in (p.y, p.up, p.down, p.far):
            o = p.at(1 - p.z, yy, p.c)
            self.arrive_parts(o)
            self.whole(o, p.partner())

    def complete(self):
        p = self.p
        for zz in (p.z, 1 - p.z):
            for yy in (p.y, p.up, p.down, p.far):
                self.arrive(p.at(zz, yy, 1 - p.c))


def kernel(
    tok_h, mod_h, wqkv1_h, wout1_h, wqkv2_h, wout2_h, wmi_h, wmo_h, out_t,
    tok_t, mod, wqkv1, wout1, wqkv2, wout2, tok, tokr, x0b, x0f, g1, g2, g3, wo1, wo2, wc1, wc2, wia, woa,
    qb, kb, vb, o1b, o1f, qkvb, o2b, o2p, o2r, xb, xp, rows_f,
    rs_send, rs_a, own_sum, mid, rs_y, res_s, res_r,
    known_x, known_z,
    tr_s, tr_r, tf_s, tf_r, o1_s, o1_r, o2_s, o2_r, re_s, re_r,
    g1_s, g1_r, g2_s, g2_r, g3_s, g3_r, w1_s, w1_r, w2_s, w2_r, wm_s, wm_r, wl_s,
    ra_s, ra_r, ry_s, ry_r,
):
    p = Place()
    s, t = p.s, p.t
    frame = jnp.bitwise_xor(s, t)
    origin = t == 0

    def rows_of(i):
        return pl.ds(pl.multiple_of(i * BLK, BLK), BLK)

    def tell(sem, dev):
        pl.semaphore_signal(sem, inc=1, device_id=dev, device_id_type=pl.DeviceIdType.MESH)

    inward = [
        pltpu.make_async_copy(src, dst, wl_s.at[j])
        for j, (src, dst) in enumerate(
            (
                (tok_h, tok_t),
                (mod_h, mod),
                (wout1_h, wout1),
                (wout2_h, wout2),
                (wqkv1_h, wqkv1),
                (wqkv2_h, wqkv2),
                (wmi_h, wia.at[0]),
                (wmo_h, woa.at[0]),
            )
        )
    ]
    for copy in inward:
        copy.start()

    barrier = pltpu.get_barrier_semaphore()
    x_peers = [(p.zh * 4 + lax.rem(p.x + j, 4), t) for j in (1, 2, 3)]
    z_peers = [(lax.rem(p.zh + j, 4) * 4 + p.x, t) for j in (1, 2, 3)]

    for dev in x_peers + z_peers + [p.z_outer()]:
        tell(barrier, dev)

    @pl.loop(1, N)
    def _(i):
        tell(barrier, (s, lax.rem(t + i, N)))

    inward[0].wait()
    rows = jnp.transpose(tok_t[...].astype(F32)).astype(BF)
    for k in range(N):
        pack(tok, k, rows[k * BLK:(k + 1) * BLK, :])
    pl.semaphore_wait(barrier, 22)

    def tok_copy(i):
        peer = lax.rem(t + i, N)
        return remote(tok.at[peer], tokr.at[t], tr_s.at[i], tr_r.at[t], (s, peer))

    @pl.loop(1, N)
    def _(i):
        tok_copy(i).start()

    tokr[t] = tok[t]
    for dev in x_peers:
        tell(known_x, dev)

    for copy in inward[1:6]:
        copy.wait()
    gw1 = WeightGather(wo1, w1_s, w1_r, p)
    gw2 = WeightGather(wo2, w2_s, w2_r, p)
    for w_in, w_all in ((wout1, wo1), (wout2, wo2)):
        w_all[t, 0:HD, :] = w_in[...]
        w_all[t, HD:PADW, :] = jnp.zeros((PADW - HD, D), BF)
    for copy in inward[6:]:
        copy.wait()
    mlp_copies = Copies(wm_s)

    def mlp_parts(parts):
        for low, size, outer in parts:
            for j, w_all in enumerate((wia, woa)):
                rows = pl.ds(low, size)
                sem = wm_r.at[j, low // 48]
                yield w_all.at[0, rows], w_all.at[1, rows], sem, p.z_outer() if outer else p.z_inner()

    def mlp_send(parts):
        for copy in mlp_parts(parts):
            mlp_copies.push(*copy)

    mlp_send(MLP_PARTS[:1])
    gw1.start_z()
    gw1.start_y(1)
    gw2.start_z()
    for w_in, w_all in ((wqkv1, wc1), (wqkv2, wc2)):
        w_all[...] = jnp.concatenate([w_in[j].astype(F32) for j in range(3)], axis=0).astype(BF)
    lanes = lax.broadcasted_iota(jnp.int32, (ROWS, 128), 1)
    vb[...] = jnp.where(lanes == HD, 1.0, 0.0).astype(BF)
    xp[...] = jnp.zeros((BLK, N * PADW), F32)

    @pl.loop(1, N)
    def _(i):
        k = lax.rem(t + i, N)
        remote(tok.at[0], tokr.at[k], tr_s.at[0], tr_r.at[k], (s, k)).wait_recv()

    def side_by_side(blocks):
        for k in range(N):
            unpack(xb, 0, k * HD, blocks, k)

    side_by_side(tokr)
    x0b[...] = xb[...].astype(BF)
    ga1 = Gather(g1, g1_s, g1_r, p, 2, 3)
    g1[rows_of(t), :] = modulated(xb[...], mod[0:1, :], mod[1:2, :])
    ga1.start()
    pl.semaphore_wait(known_x, 3)
    for dev in z_peers:
        tell(known_z, dev)
    ga1.forward()
    gw1.start_y(0)
    ga1.relay()
    pl.semaphore_wait(known_z, 3)

    def far_copy(src, dst, ss, rs, r):
        return remote(
            src.at[r], dst.at[t], ss.at[r], rs.at[t], (r, jnp.bitwise_xor(s, r))
        )

    def far_start(src, dst, ss, rs, r):
        own = jnp.logical_and(origin, r == s)

        @pl.when(jnp.logical_not(own))
        def _():
            far_copy(src, dst, ss, rs, r).start()

        @pl.when(own)
        def _():
            dst[t] = src[s]

    def far_wait_recv(src, dst, ss, rs):
        @pl.loop(0, N)
        def _(i):
            k = lax.rem(t + i, N)

            @pl.when(jnp.logical_not(jnp.logical_and(origin, i == 0)))
            def _():
                remote(
                    src.at[0], dst.at[k], ss.at[0], rs.at[k], p.partner()
                ).wait_recv()

    def far_wait_send(src, dst, ss, rs):
        @pl.loop(0, N)
        def _(r):
            @pl.when(jnp.logical_not(jnp.logical_and(origin, r == s)))
            def _():
                far_copy(src, dst, ss, rs, r).wait_send()

    corner = jnp.logical_and(s == 0, t == 0)
    row_copy = remote(x0b, x0f, tf_s, tf_r, (t, frame))

    @pl.when(jnp.logical_not(corner))
    def _():
        row_copy.start()

    @pl.when(corner)
    def _():
        x0f[...] = x0b[...]

    ga1.complete()

    @pl.loop(0, 3)
    def _(i):
        rows = pl.ds(pl.multiple_of(i * 256, 256), 256)
        r = dot_nt(g1[rows, :], wc1[...])
        qb[rows, :] = r[:, 0:HD].astype(BF)
        kb[rows, :] = r[:, HD:2 * HD].astype(BF)
        vb[rows, 0:HD] = r[:, 2 * HD:3 * HD].astype(BF)

    @pl.loop(0, 4)
    def _(i):
        part = lax.rem(i + p.zh, 4)
        rows = pl.ds(pl.multiple_of(part * 192, 192), 192)
        scores = dot_nt(qb[rows, :], kb[...])
        top = jnp.max(scores, axis=1, keepdims=True)
        raised = jnp.exp((scores - top) * SCALE).astype(BF)
        mixed = jnp.dot(raised, vb[...], preferred_element_type=F32)
        mixed = (mixed[:, 0:HD] / mixed[:, HD:HD + 1]).astype(BF)
        for j in range(4):
            pack(o1b, part * 4 + j, mixed[j * BLK:(j + 1) * BLK, :])
        for j in range(4):
            far_start(o1b, o1f, o1_s, o1_r, part * 4 + lax.rem(p.x + j, 4))

    gw2.start_y(1)
    gw2.start_y(0)
    gw1.forward()
    @pl.when(jnp.logical_not(corner))
    def _():
        row_copy.wait_recv()

    gw1.relay()
    far_wait_recv(o1b, o1f, o1_s, o1_r)
    gw1.complete()

    def project(blocks, weights):
        for k in range(N):
            unpack(xp, 0, k * PADW, blocks, k)
        return jnp.dot(
            xp[...].astype(BF), weights[...].reshape(N * PADW, D), preferred_element_type=F32
        )

    x1 = (x0f[...].astype(F32) + mod[2:3, :] * project(o1f, wo1)).astype(BF).astype(F32)
    xb[...] = x1
    ga2 = Gather(g2, g2_s, g2_r, p, 2, 3)
    g2[rows_of(t), :] = modulated(x1, mod[3:4, :], mod[4:5, :])
    ga2.start()
    ga2.forward()
    gw2.forward()
    ga2.relay()

    ga2.complete()

    @pl.loop(0, 3)
    def _(i):
        rows = pl.ds(pl.multiple_of(i * 256, 256), 256)
        qkvb[rows, :] = dot_nt(g2[rows, :], wc2[...]).astype(BF)

    same = lax.rem(lax.broadcasted_iota(jnp.int32, (256, 256), 0), 16) == lax.rem(
        lax.broadcasted_iota(jnp.int32, (256, 256), 1), 16
    )
    for grp in range(3):
        part = jnp.concatenate(
            [qkvb[f * BLK + grp * 16:f * BLK + grp * 16 + 16, :] for f in range(N)], axis=0
        )
        q, k, v = part[:, 0:HD], part[:, HD:2 * HD], part[:, 2 * HD:3 * HD]
        scores = jnp.where(same, dot_nt(q, k), -1e30)
        top = jnp.max(scores, axis=1, keepdims=True)
        raised = jnp.where(same, jnp.exp((scores - top) * SCALE), 0.0)
        weights = (raised / jnp.sum(raised, axis=1, keepdims=True)).astype(BF)
        mixed = jnp.dot(weights, v, preferred_element_type=F32).astype(BF)
        for f in range(N):
            o2b[f * BLK + grp * 16:f * BLK + grp * 16 + 16, :] = mixed[f * 16:f * 16 + 16, :]

    for f in range(N):
        pack(o2p, f, o2b[f * BLK:(f + 1) * BLK, :])

    def o2_copy(i):
        peer = lax.rem(t + i, N)
        return remote(o2p.at[peer], o2r.at[t], o2_s.at[i], o2_r.at[t], (s, peer))

    @pl.loop(1, N)
    def _(i):
        o2_copy(i).start()

    o2r[t] = o2p[t]
    mlp_send(MLP_PARTS[1:])
    gw2.relay()

    @pl.loop(1, N)
    def _(i):
        k = lax.rem(t + i, N)
        remote(o2p.at[0], o2r.at[k], o2_s.at[0], o2_r.at[k], (s, k)).wait_recv()

    gw2.complete()
    x2 = (xb[...] + mod[5:6, :] * project(o2r, wo2)).astype(BF).astype(F32)
    xb[...] = x2
    ga3 = Gather(g3, g3_s, g3_r, p, 1, 1)
    g3[rows_of(lax.rem(t, 8)), :] = modulated(x2, mod[6:7, :], mod[7:8, :])
    ga3.start()
    for src, dst, sem, _ in mlp_parts(MLP_PARTS):
        remote(src, dst, wm_s.at[0], sem, p.partner()).wait_recv()
    ga3.relay()
    ga3.complete()

    def mlp(cc):
        rows = jnp.concatenate([g3[rows_of(yy * 2 + cc), :] for yy in range(4)], axis=0)
        total = None
        for h in range(2):
            hidden = jax.nn.gelu(dot_nt(rows, wia[h]), approximate=True).astype(BF)
            term = jnp.dot(hidden, woa[h], preferred_element_type=F32)
            total = term if total is None else total + term
        return total

    def ra_copy(j):
        return remote(rs_send.at[j], rs_a.at[j], ra_s.at[j], ra_r.at[j], p.partner())

    r = mlp(1 - p.c)
    for yy in range(4):
        rs_send[yy] = r[yy * BLK:(yy + 1) * BLK, :].astype(BF)
        ra_copy(yy).start()
    r = mlp(p.c)
    for yy in range(4):
        own_sum[yy] = r[yy * BLK:(yy + 1) * BLK, :]

    def chip_sum(yy):
        ra_copy(yy).wait_recv()
        return own_sum[yy] + rs_a[yy].astype(F32)

    def ry_copy(j, yy):
        return remote(mid.at[j], rs_y.at[j], ry_s.at[j], ry_r.at[j], p.dev(p.z, yy, p.c))

    ring = (p.far, p.up, p.down)
    for j, yy in enumerate(ring):
        mid[j] = chip_sum(yy).astype(BF)
        ry_copy(j, yy).start()
    total = chip_sum(p.y)
    for j, yy in enumerate(ring):
        ry_copy(j, yy).wait_recv()
        total = total + rs_y[j].astype(F32)
    result = (xb[...] + mod[8:9, :] * total).astype(BF)
    for k in range(N):
        pack(res_s, k, result[:, k * HD:(k + 1) * HD])

    def res_copy(i):
        k = lax.rem(t + i, N)
        return remote(res_s.at[k], res_r.at[s], re_s.at[i], re_r.at[s], (frame, k))

    @pl.when(jnp.logical_not(origin))
    def _():
        res_copy(0).start()

    @pl.when(origin)
    def _():
        res_r[s] = res_s[t]

    @pl.loop(1, N)
    def _(i):
        res_copy(i).start()

    @pl.loop(1, N)
    def _(i):
        tok_copy(i).wait_send()
        o2_copy(i).wait_send()

    @pl.when(jnp.logical_not(corner))
    def _():
        row_copy.wait_send()

    far_wait_send(o1b, o1f, o1_s, o1_r)
    for g in (ga1, ga2, ga3, gw1, gw2):
        g.copies.finish()
    mlp_copies.finish()
    for yy in range(4):
        ra_copy(yy).wait_send()
    for j, yy in enumerate(ring):
        ry_copy(j, yy).wait_send()

    @pl.when(jnp.logical_not(origin))
    def _():
        res_copy(0).wait_send()
        remote(res_s.at[0], res_r.at[s], re_s.at[0], re_r.at[s], p.partner()).wait_recv()

    @pl.loop(1, N)
    def _(i):
        res_copy(i).wait_send()
        k = lax.rem(s + i, N)
        remote(res_s.at[0], res_r.at[k], re_s.at[0], re_r.at[k], p.partner()).wait_recv()

    for k in range(N):
        unpack(rows_f, k * BLK, 0, res_r, k)
    out_t[...] = jnp.transpose(rows_f[...]).astype(BF)


def per_device(tokens, modulation, spatial_qkv, spatial_out, temporal_qkv, temporal_out, mlp_in, mlp_out):
    vm = pltpu.VMEM
    dma = pltpu.SemaphoreType.DMA
    regular = pltpu.SemaphoreType.REGULAR
    scratch = [
        vm((HD, ROWS), BF),
        vm((9, D), F32),
        vm((3, HD, D), BF),
        vm((HD, D), BF),
        vm((3, HD, D), BF),
        vm((HD, D), BF),
        vm((N, PK, 128), BF),
        vm((N, PK, 128), BF),
        vm((BLK, D), BF),
        vm((BLK, D), BF),
        vm((ROWS, D), BF),
        vm((ROWS, D), BF),
        vm((ROWS // 2, D), BF),
        vm((N, PADW, D), BF),
        vm((N, PADW, D), BF),
        vm((3 * HD, D), BF),
        vm((3 * HD, D), BF),
        vm((2, FFL, D), BF),
        vm((2, FFL, D), BF),
        vm((ROWS, HD), BF),
        vm((ROWS, HD), BF),
        vm((ROWS, 128), BF),
        vm((N, PK, 128), BF),
        vm((N, PK, 128), BF),
        vm((ROWS, 3 * HD), BF),
        vm((ROWS, HD), BF),
        vm((N, PK, 128), BF),
        vm((N, PK, 128), BF),
        vm((BLK, D), F32),
        vm((BLK, N * PADW), F32),
        vm((ROWS, HD), F32),
        vm((4, BLK, D), BF),
        vm((4, BLK, D), BF),
        vm((4, BLK, D), F32),
        vm((3, BLK, D), BF),
        vm((3, BLK, D), BF),
        vm((N, PK, 128), BF),
        vm((N, PK, 128), BF),
        regular,
        regular,
    ]
    scratch += [dma((N,))] * 2 + [dma, dma] + [dma((N,))] * 6
    scratch += [dma((64,)), dma((N, 3))] * 3
    scratch += [dma((24,)), dma((N, 2))] * 2
    scratch += [dma((6,)), dma((2, 6)), dma((8,))]
    scratch += [dma((4,)), dma((4,)), dma((3,)), dma((3,))]
    return pl.pallas_call(
        kernel,
        out_shape=jax.ShapeDtypeStruct((HD, ROWS), BF),
        in_specs=[pl.BlockSpec(memory_space=pltpu.HBM)] * 8,
        out_specs=pl.BlockSpec(memory_space=pltpu.VMEM),
        scratch_shapes=scratch,
        compiler_params=pltpu.CompilerParams(
            collective_id=0, has_side_effects=True, vmem_limit_bytes=60 * 1024 * 1024
        ),
        cost_estimate=pl.CostEstimate(
            flops=2_300_000_000, bytes_accessed=4_000_000, transcendentals=1_000_000
        ),
    )(
        tokens.T,
        modulation,
        jnp.swapaxes(spatial_qkv, 1, 2),
        spatial_out,
        jnp.swapaxes(temporal_qkv, 1, 2),
        temporal_out,
        mlp_in.T,
        mlp_out,
    ).T


def solution(mesh):
    return jax.shard_map(
        per_device,
        mesh=mesh,
        in_specs=(
            P("seq", "tp"),
            P(),
            P(None, None, "tp"),
            P("tp", None),
            P(None, None, "tp"),
            P("tp", None),
            P(None, "tp"),
            P("tp", None),
        ),
        out_specs=P("seq", "tp"),
        check_vma=False,
    )
```

```python
import jax
import jax.numpy as jnp
from jax import lax
from jax.experimental import pallas as pl
from jax.experimental.pallas import tpu as pltpu
from jax.sharding import PartitionSpec as P

HD = 72
D = 1152
N = 16
ROWS = 768
BLK = 48
PK = 32
FFL = 288
PADW = 80
CUT = 48
MLP_PARTS = ((0, 144, True), (144, 64, True), (208, 80, False))
EPS = 1e-06
SCALE = HD ** (-0.5)
BF = jnp.bfloat16
F32 = jnp.float32


def remote(src, dst, send_sem, recv_sem, device):
    return pltpu.make_async_remote_copy(
        src_ref=src,
        dst_ref=dst,
        send_sem=send_sem,
        recv_sem=recv_sem,
        device_id=device,
        device_id_type=pl.DeviceIdType.MESH,
    )


def dot_nt(a, b):
    return lax.dot_general(a, b, (((1,), (1,)), ((), ())), preferred_element_type=F32)


def modulated(rows, shift, scale):
    average = jnp.mean(rows, axis=-1, keepdims=True)
    centred = rows - average
    variance = jnp.mean(centred * centred, axis=-1, keepdims=True)
    return (centred * lax.rsqrt(variance + EPS) * (1.0 + scale) + shift).astype(BF)


def pack(dst, i, block):
    dst[i, :, 0:HD] = block[0:PK, :]
    dst[i, 0:16, HD:128] = block[PK:BLK, 0:128 - HD]
    dst[i, 16:PK, HD:2 * HD - 56] = block[PK:BLK, 56:HD]


def unpack(dst, row, low, src, i):
    block = src[i].astype(F32)
    dst[row:row + PK, low:low + HD] = block[:, 0:HD]
    dst[row + PK:row + BLK, low:low + 56] = block[0:16, HD:128]
    dst[row + PK:row + BLK, low + 56:low + HD] = block[16:PK, HD:2 * HD - 56]


class Copies:
    def __init__(self, send):
        self.send = send
        self.started = []

    def push(self, src, dst, recv, device):
        copy = remote(src, dst, self.send.at[len(self.started)], recv, device)
        copy.start()
        self.started.append(copy)

    def finish(self):
        for copy in self.started:
            copy.wait_send()


class Place:
    def __init__(self):
        self.s = lax.axis_index("seq")
        self.t = lax.axis_index("tp")
        self.z = lax.div(self.t, 8)
        self.y = lax.rem(lax.div(self.t, 2), 4)
        self.c = lax.rem(self.t, 2)
        self.zh = lax.div(self.s, 4)
        self.x = lax.rem(self.s, 4)
        self.up = lax.rem(self.y + 1, 4)
        self.down = lax.rem(self.y + 3, 4)
        self.far = lax.rem(self.y + 2, 4)

    def at(self, z, y, c):
        return z * 8 + y * 2 + c

    def dev(self, z, y, c):
        return (self.s, self.at(z, y, c))

    def partner(self):
        return self.dev(self.z, self.y, 1 - self.c)

    def z_inner(self):
        return self.dev(1 - self.z, self.y, self.c)

    def z_outer(self):
        zh = lax.rem(self.zh + jnp.where(self.z == 1, 1, 3), 4)
        return (zh * 4 + self.x, self.at(1 - self.z, self.y, self.c))


class Gather:
    def __init__(self, buf, send, recv, at, planes, chunks):
        self.buf, self.recv, self.p, self.planes, self.chunks = buf, recv, at, planes, chunks
        self.rows = BLK // chunks
        self.copies = Copies(send)

    def slot(self, o, k):
        if self.planes == 1:
            o = lax.rem(o, 8)
        return self.buf.at[pl.ds(pl.multiple_of(o * BLK + k * self.rows, self.rows), self.rows)]

    def sem(self, o, k):
        return self.recv.at[o, k]

    def push(self, o, k, device):
        ref = self.slot(o, k)
        self.copies.push(ref, ref, self.sem(o, k), device)

    def arrive(self, o, k):
        ref = self.slot(o, k)
        remote(ref, ref, self.copies.send.at[0], self.sem(o, k), self.p.partner()).wait_recv()

    def start(self):
        p = self.p
        for k in range(self.chunks):
            if self.planes == 2:
                self.push(p.t, k, p.z_inner())
            for yy in (p.up, p.down, p.far):
                self.push(p.t, k, p.dev(p.z, yy, p.c))
        for k in range(self.chunks):
            self.push(p.t, k, p.partner())

    def forward(self):
        p = self.p
        if self.planes == 1:
            return
        for k in range(self.chunks):
            o = p.at(1 - p.z, p.y, p.c)
            self.arrive(o, k)
            for yy in (p.up, p.down):
                self.push(o, k, p.dev(p.z, yy, p.c))
            self.push(o, k, p.partner())
        for k in range(self.chunks):
            o = p.at(p.z, p.far, p.c)
            self.arrive(o, k)
            self.push(o, k, p.z_inner())
            self.push(o, k, p.partner())

    def relay(self):
        p = self.p
        near = (p.up, p.down) if self.planes == 2 else (p.up, p.down, p.far)
        for k in range(self.chunks):
            for yy in near:
                o = p.at(p.z, yy, p.c)
                self.arrive(o, k)
                self.push(o, k, p.partner())
        if self.planes == 2:
            for k in range(self.chunks):
                for yy in (p.up, p.down, p.far):
                    o = p.at(1 - p.z, yy, p.c)
                    self.arrive(o, k)
                    self.push(o, k, p.partner())

    def complete(self):
        p = self.p
        for zz in (p.z, 1 - p.z)[: self.planes]:
            for yy in (p.y, p.up, p.down, p.far):
                for k in range(self.chunks):
                    self.arrive(p.at(zz, yy, 1 - p.c), k)


class WeightGather:
    def __init__(self, buf, send, recv, at):
        self.buf, self.recv, self.p = buf, recv, at
        self.copies = Copies(send)

    def part(self, o, h):
        return self.buf.at[o, pl.ds(0, CUT)] if h == 0 else self.buf.at[o, pl.ds(CUT, PADW - CUT)]

    def halves(self, o):
        p = self.p
        for h, device in ((0, p.z_inner()), (1, p.z_outer())):
            ref = self.part(o, h)
            self.copies.push(ref, ref, self.recv.at[o, h], device)

    def whole(self, o, device):
        ref = self.buf.at[o]
        self.copies.push(ref, ref, self.recv.at[o, 0], device)

    def arrive(self, o):
        ref = self.buf.at[o]
        remote(ref, ref, self.copies.send.at[0], self.recv.at[o, 0], self.p.partner()).wait_recv()

    def arrive_parts(self, o):
        for h in range(2):
            ref = self.part(o, h)
            remote(
                ref, ref, self.copies.send.at[0], self.recv.at[o, h], self.p.partner()
            ).wait_recv()

    def start_z(self):
        self.halves(self.p.t)

    def start_y(self, h):
        p = self.p
        ref = self.part(p.t, h)
        for yy in (p.far, p.up, p.down):
            self.copies.push(ref, ref, self.recv.at[p.t, h], p.dev(p.z, yy, p.c))
        if h == 0:
            self.whole(p.t, p.partner())

    def forward(self):
        p = self.p
        for yy in (p.up, p.down, p.far):
            o = p.at(p.z, yy, p.c)
            self.arrive_parts(o)
            self.halves(o)
            self.whole(o, p.partner())

    def relay(self):
        p = self.p
        for yy in (p.y, p.up, p.down, p.far):
            o = p.at(1 - p.z, yy, p.c)
            self.arrive_parts(o)
            self.whole(o, p.partner())

    def complete(self):
        p = self.p
        for zz in (p.z, 1 - p.z):
            for yy in (p.y, p.up, p.down, p.far):
                self.arrive(p.at(zz, yy, 1 - p.c))


def kernel(
    tok_h, mod_h, wqkv1_h, wout1_h, wqkv2_h, wout2_h, wmi_h, wmo_h, out_t,
    tok_t, mod, wqkv1, wout1, wqkv2, wout2, tok, tokr, x0b, x0f, g1, g2, g3, wo1, wo2, wc1, wc2, wia, woa,
    qb, kb, vb, o1b, o1f, qkvb, o2b, o2p, o2r, xb, xp, rows_f,
    rs_send, rs_a, own_sum, mid, rs_y, res_s, res_r,
    known_x, known_z,
    tr_s, tr_r, tf_s, tf_r, o1_s, o1_r, o2_s, o2_r, re_s, re_r,
    g1_s, g1_r, g2_s, g2_r, g3_s, g3_r, w1_s, w1_r, w2_s, w2_r, wm_s, wm_r, wl_s,
    ra_s, ra_r, ry_s, ry_r,
):
    p = Place()
    s, t = p.s, p.t
    frame = jnp.bitwise_xor(s, t)
    origin = t == 0

    def rows_of(i):
        return pl.ds(pl.multiple_of(i * BLK, BLK), BLK)

    def tell(sem, dev):
        pl.semaphore_signal(sem, inc=1, device_id=dev, device_id_type=pl.DeviceIdType.MESH)

    inward = [
        pltpu.make_async_copy(src, dst, wl_s.at[j])
        for j, (src, dst) in enumerate(
            (
                (tok_h, tok_t),
                (mod_h, mod),
                (wout1_h, wout1),
                (wout2_h, wout2),
                (wqkv1_h, wqkv1),
                (wqkv2_h, wqkv2),
                (wmi_h, wia.at[0]),
                (wmo_h, woa.at[0]),
            )
        )
    ]
    for copy in inward:
        copy.start()

    barrier = pltpu.get_barrier_semaphore()
    x_peers = [(p.zh * 4 + lax.rem(p.x + j, 4), t) for j in (1, 2, 3)]
    z_peers = [(lax.rem(p.zh + j, 4) * 4 + p.x, t) for j in (1, 2, 3)]

    for dev in x_peers + z_peers + [p.z_outer()]:
        tell(barrier, dev)

    @pl.loop(1, N)
    def _(i):
        tell(barrier, (s, lax.rem(t + i, N)))

    inward[0].wait()
    rows = jnp.transpose(tok_t[...].astype(F32)).astype(BF)
    for k in range(N):
        pack(tok, k, rows[k * BLK:(k + 1) * BLK, :])
    pl.semaphore_wait(barrier, 22)

    def tok_copy(i):
        peer = lax.rem(t + i, N)
        return remote(tok.at[peer], tokr.at[t], tr_s.at[i], tr_r.at[t], (s, peer))

    @pl.loop(1, N)
    def _(i):
        tok_copy(i).start()

    tokr[t] = tok[t]
    for dev in x_peers:
        tell(known_x, dev)

    for copy in inward[1:6]:
        copy.wait()
    gw1 = WeightGather(wo1, w1_s, w1_r, p)
    gw2 = WeightGather(wo2, w2_s, w2_r, p)
    for w_in, w_all in ((wout1, wo1), (wout2, wo2)):
        w_all[t, 0:HD, :] = w_in[...]
        w_all[t, HD:PADW, :] = jnp.zeros((PADW - HD, D), BF)
    for copy in inward[6:]:
        copy.wait()
    mlp_copies = Copies(wm_s)

    def mlp_parts(parts):
        for low, size, outer in parts:
            for j, w_all in enumerate((wia, woa)):
                rows = pl.ds(low, size)
                sem = wm_r.at[j, low // 48]
                yield w_all.at[0, rows], w_all.at[1, rows], sem, p.z_outer() if outer else p.z_inner()

    def mlp_send(parts):
        for copy in mlp_parts(parts):
            mlp_copies.push(*copy)

    gw1.start_z()
    gw1.start_y(1)
    gw2.start_z()
    mlp_send(MLP_PARTS[:1])
    for w_in, w_all in ((wqkv1, wc1), (wqkv2, wc2)):
        w_all[...] = jnp.concatenate([w_in[j].astype(F32) for j in range(3)], axis=0).astype(BF)
    lanes = lax.broadcasted_iota(jnp.int32, (ROWS, 128), 1)
    vb[...] = jnp.where(lanes == HD, 1.0, 0.0).astype(BF)
    xp[...] = jnp.zeros((BLK, N * PADW), F32)

    @pl.loop(1, N)
    def _(i):
        k = lax.rem(t + i, N)
        remote(tok.at[0], tokr.at[k], tr_s.at[0], tr_r.at[k], (s, k)).wait_recv()

    def side_by_side(blocks):
        for k in range(N):
            unpack(xb, 0, k * HD, blocks, k)

    side_by_side(tokr)
    x0b[...] = xb[...].astype(BF)
    ga1 = Gather(g1, g1_s, g1_r, p, 2, 3)
    g1[rows_of(t), :] = modulated(xb[...], mod[0:1, :], mod[1:2, :])
    ga1.start()
    pl.semaphore_wait(known_x, 3)
    for dev in z_peers:
        tell(known_z, dev)
    ga1.forward()
    gw1.start_y(0)
    ga1.relay()
    pl.semaphore_wait(known_z, 3)

    def far_copy(src, dst, ss, rs, r):
        return remote(
            src.at[r], dst.at[t], ss.at[r], rs.at[t], (r, jnp.bitwise_xor(s, r))
        )

    def far_start(src, dst, ss, rs, r):
        own = jnp.logical_and(origin, r == s)

        @pl.when(jnp.logical_not(own))
        def _():
            far_copy(src, dst, ss, rs, r).start()

        @pl.when(own)
        def _():
            dst[t] = src[s]

    def far_wait_recv(src, dst, ss, rs):
        @pl.loop(0, N)
        def _(i):
            k = lax.rem(t + i, N)

            @pl.when(jnp.logical_not(jnp.logical_and(origin, i == 0)))
            def _():
                remote(
                    src.at[0], dst.at[k], ss.at[0], rs.at[k], p.partner()
                ).wait_recv()

    def far_wait_send(src, dst, ss, rs):
        @pl.loop(0, N)
        def _(r):
            @pl.when(jnp.logical_not(jnp.logical_and(origin, r == s)))
            def _():
                far_copy(src, dst, ss, rs, r).wait_send()

    corner = jnp.logical_and(s == 0, t == 0)
    row_copy = remote(x0b, x0f, tf_s, tf_r, (t, frame))

    @pl.when(jnp.logical_not(corner))
    def _():
        row_copy.start()

    @pl.when(corner)
    def _():
        x0f[...] = x0b[...]

    ga1.complete()

    @pl.loop(0, 3)
    def _(i):
        rows = pl.ds(pl.multiple_of(i * 256, 256), 256)
        r = dot_nt(g1[rows, :], wc1[...])
        qb[rows, :] = r[:, 0:HD].astype(BF)
        kb[rows, :] = r[:, HD:2 * HD].astype(BF)
        vb[rows, 0:HD] = r[:, 2 * HD:3 * HD].astype(BF)

    @pl.loop(0, 4)
    def _(i):
        part = lax.rem(i + p.zh, 4)
        rows = pl.ds(pl.multiple_of(part * 192, 192), 192)
        scores = dot_nt(qb[rows, :], kb[...])
        top = jnp.max(scores, axis=1, keepdims=True)
        raised = jnp.exp((scores - top) * SCALE).astype(BF)
        mixed = jnp.dot(raised, vb[...], preferred_element_type=F32)
        mixed = (mixed[:, 0:HD] / mixed[:, HD:HD + 1]).astype(BF)
        for j in range(4):
            pack(o1b, part * 4 + j, mixed[j * BLK:(j + 1) * BLK, :])
        for j in range(4):
            far_start(o1b, o1f, o1_s, o1_r, part * 4 + lax.rem(p.x + j, 4))

    gw2.start_y(1)
    gw2.start_y(0)
    gw1.forward()
    @pl.when(jnp.logical_not(corner))
    def _():
        row_copy.wait_recv()

    gw1.relay()
    far_wait_recv(o1b, o1f, o1_s, o1_r)
    gw1.complete()

    def project(blocks, weights):
        for k in range(N):
            unpack(xp, 0, k * PADW, blocks, k)
        return jnp.dot(
            xp[...].astype(BF), weights[...].reshape(N * PADW, D), preferred_element_type=F32
        )

    x1 = (x0f[...].astype(F32) + mod[2:3, :] * project(o1f, wo1)).astype(BF).astype(F32)
    xb[...] = x1
    ga2 = Gather(g2, g2_s, g2_r, p, 2, 3)
    g2[rows_of(t), :] = modulated(x1, mod[3:4, :], mod[4:5, :])
    ga2.start()
    ga2.forward()
    gw2.forward()
    ga2.relay()

    ga2.complete()

    @pl.loop(0, 3)
    def _(i):
        rows = pl.ds(pl.multiple_of(i * 256, 256), 256)
        qkvb[rows, :] = dot_nt(g2[rows, :], wc2[...]).astype(BF)

    same = lax.rem(lax.broadcasted_iota(jnp.int32, (256, 256), 0), 16) == lax.rem(
        lax.broadcasted_iota(jnp.int32, (256, 256), 1), 16
    )
    for grp in range(3):
        part = jnp.concatenate(
            [qkvb[f * BLK + grp * 16:f * BLK + grp * 16 + 16, :] for f in range(N)], axis=0
        )
        q, k, v = part[:, 0:HD], part[:, HD:2 * HD], part[:, 2 * HD:3 * HD]
        scores = jnp.where(same, dot_nt(q, k), -1e30)
        top = jnp.max(scores, axis=1, keepdims=True)
        raised = jnp.where(same, jnp.exp((scores - top) * SCALE), 0.0)
        weights = (raised / jnp.sum(raised, axis=1, keepdims=True)).astype(BF)
        mixed = jnp.dot(weights, v, preferred_element_type=F32).astype(BF)
        for f in range(N):
            o2b[f * BLK + grp * 16:f * BLK + grp * 16 + 16, :] = mixed[f * 16:f * 16 + 16, :]

    for f in range(N):
        pack(o2p, f, o2b[f * BLK:(f + 1) * BLK, :])

    def o2_copy(i):
        peer = lax.rem(t + i, N)
        return remote(o2p.at[peer], o2r.at[t], o2_s.at[i], o2_r.at[t], (s, peer))

    @pl.loop(1, N)
    def _(i):
        o2_copy(i).start()

    o2r[t] = o2p[t]
    mlp_send(MLP_PARTS[1:])
    gw2.relay()

    @pl.loop(1, N)
    def _(i):
        k = lax.rem(t + i, N)
        remote(o2p.at[0], o2r.at[k], o2_s.at[0], o2_r.at[k], (s, k)).wait_recv()

    gw2.complete()
    x2 = (xb[...] + mod[5:6, :] * project(o2r, wo2)).astype(BF).astype(F32)
    xb[...] = x2
    ga3 = Gather(g3, g3_s, g3_r, p, 1, 3)
    g3[rows_of(lax.rem(t, 8)), :] = modulated(x2, mod[6:7, :], mod[7:8, :])
    ga3.start()
    for src, dst, sem, _ in mlp_parts(MLP_PARTS):
        remote(src, dst, wm_s.at[0], sem, p.partner()).wait_recv()
    ga3.relay()
    ga3.complete()

    def mlp(cc):
        rows = jnp.concatenate([g3[rows_of(yy * 2 + cc), :] for yy in range(4)], axis=0)
        total = None
        for h in range(2):
            hidden = jax.nn.gelu(dot_nt(rows, wia[h]), approximate=True).astype(BF)
            term = jnp.dot(hidden, woa[h], preferred_element_type=F32)
            total = term if total is None else total + term
        return total

    def ra_copy(j):
        return remote(rs_send.at[j], rs_a.at[j], ra_s.at[j], ra_r.at[j], p.partner())

    r = mlp(1 - p.c)
    for yy in range(4):
        rs_send[yy] = r[yy * BLK:(yy + 1) * BLK, :].astype(BF)
        ra_copy(yy).start()
    r = mlp(p.c)
    for yy in range(4):
        own_sum[yy] = r[yy * BLK:(yy + 1) * BLK, :]

    def chip_sum(yy):
        ra_copy(yy).wait_recv()
        return own_sum[yy] + rs_a[yy].astype(F32)

    def ry_copy(j, yy):
        return remote(mid.at[j], rs_y.at[j], ry_s.at[j], ry_r.at[j], p.dev(p.z, yy, p.c))

    ring = (p.far, p.up, p.down)
    for j, yy in enumerate(ring):
        mid[j] = chip_sum(yy).astype(BF)
        ry_copy(j, yy).start()
    total = chip_sum(p.y)
    for j, yy in enumerate(ring):
        ry_copy(j, yy).wait_recv()
        total = total + rs_y[j].astype(F32)
    result = (xb[...] + mod[8:9, :] * total).astype(BF)
    for k in range(N):
        pack(res_s, k, result[:, k * HD:(k + 1) * HD])

    def res_copy(i):
        k = lax.rem(t + i, N)
        return remote(res_s.at[k], res_r.at[s], re_s.at[i], re_r.at[s], (frame, k))

    @pl.when(jnp.logical_not(origin))
    def _():
        res_copy(0).start()

    @pl.when(origin)
    def _():
        res_r[s] = res_s[t]

    @pl.loop(1, N)
    def _(i):
        res_copy(i).start()

    @pl.loop(1, N)
    def _(i):
        tok_copy(i).wait_send()
        o2_copy(i).wait_send()

    @pl.when(jnp.logical_not(corner))
    def _():
        row_copy.wait_send()

    far_wait_send(o1b, o1f, o1_s, o1_r)
    for g in (ga1, ga2, ga3, gw1, gw2):
        g.copies.finish()
    mlp_copies.finish()
    for yy in range(4):
        ra_copy(yy).wait_send()
    for j, yy in enumerate(ring):
        ry_copy(j, yy).wait_send()

    @pl.when(jnp.logical_not(origin))
    def _():
        res_copy(0).wait_send()
        remote(res_s.at[0], res_r.at[s], re_s.at[0], re_r.at[s], p.partner()).wait_recv()

    @pl.loop(1, N)
    def _(i):
        res_copy(i).wait_send()
        k = lax.rem(s + i, N)
        remote(res_s.at[0], res_r.at[k], re_s.at[0], re_r.at[k], p.partner()).wait_recv()

    for k in range(N):
        unpack(rows_f, k * BLK, 0, res_r, k)
    out_t[...] = jnp.transpose(rows_f[...]).astype(BF)


def per_device(tokens, modulation, spatial_qkv, spatial_out, temporal_qkv, temporal_out, mlp_in, mlp_out):
    vm = pltpu.VMEM
    dma = pltpu.SemaphoreType.DMA
    regular = pltpu.SemaphoreType.REGULAR
    scratch = [
        vm((HD, ROWS), BF),
        vm((9, D), F32),
        vm((3, HD, D), BF),
        vm((HD, D), BF),
        vm((3, HD, D), BF),
        vm((HD, D), BF),
        vm((N, PK, 128), BF),
        vm((N, PK, 128), BF),
        vm((BLK, D), BF),
        vm((BLK, D), BF),
        vm((ROWS, D), BF),
        vm((ROWS, D), BF),
        vm((ROWS // 2, D), BF),
        vm((N, PADW, D), BF),
        vm((N, PADW, D), BF),
        vm((3 * HD, D), BF),
        vm((3 * HD, D), BF),
        vm((2, FFL, D), BF),
        vm((2, FFL, D), BF),
        vm((ROWS, HD), BF),
        vm((ROWS, HD), BF),
        vm((ROWS, 128), BF),
        vm((N, PK, 128), BF),
        vm((N, PK, 128), BF),
        vm((ROWS, 3 * HD), BF),
        vm((ROWS, HD), BF),
        vm((N, PK, 128), BF),
        vm((N, PK, 128), BF),
        vm((BLK, D), F32),
        vm((BLK, N * PADW), F32),
        vm((ROWS, HD), F32),
        vm((4, BLK, D), BF),
        vm((4, BLK, D), BF),
        vm((4, BLK, D), F32),
        vm((3, BLK, D), BF),
        vm((3, BLK, D), BF),
        vm((N, PK, 128), BF),
        vm((N, PK, 128), BF),
        regular,
        regular,
    ]
    scratch += [dma((N,))] * 2 + [dma, dma] + [dma((N,))] * 6
    scratch += [dma((64,)), dma((N, 3))] * 3
    scratch += [dma((24,)), dma((N, 2))] * 2
    scratch += [dma((6,)), dma((2, 6)), dma((8,))]
    scratch += [dma((4,)), dma((4,)), dma((3,)), dma((3,))]
    return pl.pallas_call(
        kernel,
        out_shape=jax.ShapeDtypeStruct((HD, ROWS), BF),
        in_specs=[pl.BlockSpec(memory_space=pltpu.HBM)] * 8,
        out_specs=pl.BlockSpec(memory_space=pltpu.VMEM),
        scratch_shapes=scratch,
        compiler_params=pltpu.CompilerParams(
            collective_id=0, has_side_effects=True, vmem_limit_bytes=60 * 1024 * 1024
        ),
        cost_estimate=pl.CostEstimate(
            flops=2_300_000_000, bytes_accessed=4_000_000, transcendentals=1_000_000
        ),
    )(
        tokens.T,
        modulation,
        jnp.swapaxes(spatial_qkv, 1, 2),
        spatial_out,
        jnp.swapaxes(temporal_qkv, 1, 2),
        temporal_out,
        mlp_in.T,
        mlp_out,
    ).T


def solution(mesh):
    return jax.shard_map(
        per_device,
        mesh=mesh,
        in_specs=(
            P("seq", "tp"),
            P(),
            P(None, None, "tp"),
            P("tp", None),
            P(None, None, "tp"),
            P("tp", None),
            P(None, "tp"),
            P("tp", None),
        ),
        out_specs=P("seq", "tp"),
        check_vma=False,
    )
```

```python
import jax
import jax.numpy as jnp
from jax import lax
from jax.experimental import pallas as pl
from jax.experimental.pallas import tpu as pltpu
from jax.sharding import PartitionSpec as P

HD = 72
D = 1152
N = 16
ROWS = 768
BLK = 48
PK = 32
FFL = 288
PADW = 80
CUT = 48
MLP_PARTS = ((0, 144, True), (144, 64, True), (208, 80, False))
EPS = 1e-06
SCALE = HD ** (-0.5)
BF = jnp.bfloat16
F32 = jnp.float32


def remote(src, dst, send_sem, recv_sem, device):
    return pltpu.make_async_remote_copy(
        src_ref=src,
        dst_ref=dst,
        send_sem=send_sem,
        recv_sem=recv_sem,
        device_id=device,
        device_id_type=pl.DeviceIdType.MESH,
    )


def dot_nt(a, b):
    return lax.dot_general(a, b, (((1,), (1,)), ((), ())), preferred_element_type=F32)


def modulated(rows, shift, scale):
    average = jnp.mean(rows, axis=-1, keepdims=True)
    centred = rows - average
    variance = jnp.mean(centred * centred, axis=-1, keepdims=True)
    return (centred * lax.rsqrt(variance + EPS) * (1.0 + scale) + shift).astype(BF)


def pack(dst, i, block):
    dst[i, :, 0:HD] = block[0:PK, :]
    dst[i, 0:16, HD:128] = block[PK:BLK, 0:128 - HD]
    dst[i, 16:PK, HD:2 * HD - 56] = block[PK:BLK, 56:HD]


def unpack(dst, row, low, src, i):
    block = src[i].astype(F32)
    dst[row:row + PK, low:low + HD] = block[:, 0:HD]
    dst[row + PK:row + BLK, low:low + 56] = block[0:16, HD:128]
    dst[row + PK:row + BLK, low + 56:low + HD] = block[16:PK, HD:2 * HD - 56]


class Copies:
    def __init__(self, send):
        self.send = send
        self.started = []

    def push(self, src, dst, recv, device):
        copy = remote(src, dst, self.send.at[len(self.started)], recv, device)
        copy.start()
        self.started.append(copy)

    def finish(self):
        for copy in self.started:
            copy.wait_send()


class Place:
    def __init__(self):
        self.s = lax.axis_index("seq")
        self.t = lax.axis_index("tp")
        self.z = lax.div(self.t, 8)
        self.y = lax.rem(lax.div(self.t, 2), 4)
        self.c = lax.rem(self.t, 2)
        self.zh = lax.div(self.s, 4)
        self.x = lax.rem(self.s, 4)
        self.up = lax.rem(self.y + 1, 4)
        self.down = lax.rem(self.y + 3, 4)
        self.far = lax.rem(self.y + 2, 4)

    def at(self, z, y, c):
        return z * 8 + y * 2 + c

    def dev(self, z, y, c):
        return (self.s, self.at(z, y, c))

    def partner(self):
        return self.dev(self.z, self.y, 1 - self.c)

    def z_inner(self):
        return self.dev(1 - self.z, self.y, self.c)

    def z_outer(self):
        zh = lax.rem(self.zh + jnp.where(self.z == 1, 1, 3), 4)
        return (zh * 4 + self.x, self.at(1 - self.z, self.y, self.c))


class Gather:
    def __init__(self, buf, send, recv, at, planes, chunks):
        self.buf, self.recv, self.p, self.planes, self.chunks = buf, recv, at, planes, chunks
        self.rows = BLK // chunks
        self.copies = Copies(send)

    def slot(self, o, k):
        if self.planes == 1:
            o = lax.rem(o, 8)
        return self.buf.at[pl.ds(pl.multiple_of(o * BLK + k * self.rows, self.rows), self.rows)]

    def sem(self, o, k):
        return self.recv.at[o, k]

    def push(self, o, k, device):
        ref = self.slot(o, k)
        self.copies.push(ref, ref, self.sem(o, k), device)

    def arrive(self, o, k):
        ref = self.slot(o, k)
        remote(ref, ref, self.copies.send.at[0], self.sem(o, k), self.p.partner()).wait_recv()

    def start(self):
        p = self.p
        for k in range(self.chunks):
            if self.planes == 2:
                self.push(p.t, k, p.z_inner())
            for yy in (p.up, p.down, p.far):
                self.push(p.t, k, p.dev(p.z, yy, p.c))
        for k in range(self.chunks):
            self.push(p.t, k, p.partner())

    def forward(self):
        p = self.p
        if self.planes == 1:
            return
        for k in range(self.chunks):
            o = p.at(1 - p.z, p.y, p.c)
            self.arrive(o, k)
            for yy in (p.up, p.down):
                self.push(o, k, p.dev(p.z, yy, p.c))
            self.push(o, k, p.partner())
        for k in range(self.chunks):
            o = p.at(p.z, p.far, p.c)
            self.arrive(o, k)
            self.push(o, k, p.z_inner())
            self.push(o, k, p.partner())

    def relay(self):
        p = self.p
        near = (p.up, p.down) if self.planes == 2 else (p.up, p.down, p.far)
        for k in range(self.chunks):
            for yy in near:
                o = p.at(p.z, yy, p.c)
                self.arrive(o, k)
                self.push(o, k, p.partner())
        if self.planes == 2:
            for k in range(self.chunks):
                for yy in (p.up, p.down, p.far):
                    o = p.at(1 - p.z, yy, p.c)
                    self.arrive(o, k)
                    self.push(o, k, p.partner())

    def complete(self):
        p = self.p
        for zz in (p.z, 1 - p.z)[: self.planes]:
            for yy in (p.y, p.up, p.down, p.far):
                for k in range(self.chunks):
                    self.arrive(p.at(zz, yy, 1 - p.c), k)


class WeightGather:
    def __init__(self, buf, send, recv, at):
        self.buf, self.recv, self.p = buf, recv, at
        self.copies = Copies(send)

    def part(self, o, h):
        return self.buf.at[o, pl.ds(0, CUT)] if h == 0 else self.buf.at[o, pl.ds(CUT, PADW - CUT)]

    def halves(self, o):
        p = self.p
        for h, device in ((0, p.z_inner()), (1, p.z_outer())):
            ref = self.part(o, h)
            self.copies.push(ref, ref, self.recv.at[o, h], device)

    def whole(self, o, device):
        ref = self.buf.at[o]
        self.copies.push(ref, ref, self.recv.at[o, 0], device)

    def arrive(self, o):
        ref = self.buf.at[o]
        remote(ref, ref, self.copies.send.at[0], self.recv.at[o, 0], self.p.partner()).wait_recv()

    def arrive_parts(self, o):
        for h in range(2):
            ref = self.part(o, h)
            remote(
                ref, ref, self.copies.send.at[0], self.recv.at[o, h], self.p.partner()
            ).wait_recv()

    def start_z(self):
        self.halves(self.p.t)

    def start_y(self, h):
        p = self.p
        ref = self.part(p.t, h)
        for yy in (p.far, p.up, p.down):
            self.copies.push(ref, ref, self.recv.at[p.t, h], p.dev(p.z, yy, p.c))
        if h == 0:
            self.whole(p.t, p.partner())

    def forward(self):
        p = self.p
        for yy in (p.up, p.down, p.far):
            o = p.at(p.z, yy, p.c)
            self.arrive_parts(o)
            self.halves(o)
            self.whole(o, p.partner())

    def relay(self):
        p = self.p
        for yy in (p.y, p.up, p.down, p.far):
            o = p.at(1 - p.z, yy, p.c)
            self.arrive_parts(o)
            self.whole(o, p.partner())

    def complete(self):
        p = self.p
        for zz in (p.z, 1 - p.z):
            for yy in (p.y, p.up, p.down, p.far):
                self.arrive(p.at(zz, yy, 1 - p.c))


def kernel(
    tok_h, mod_h, wqkv1_h, wout1_h, wqkv2_h, wout2_h, wmi_h, wmo_h, out_t,
    tok_t, mod, wqkv1, wout1, wqkv2, wout2, tok, tokr, x0b, x0f, g1, g2, g3, wo1, wo2, wc1, wc2, wia, woa,
    qb, kb, vb, o1b, o1f, qkvb, o2b, o2p, o2r, xb, xp, rows_f,
    rs_send, rs_a, own_sum, mid, rs_y, res_s, res_r,
    known_x, known_z,
    tr_s, tr_r, tf_s, tf_r, o1_s, o1_r, o2_s, o2_r, re_s, re_r,
    g1_s, g1_r, g2_s, g2_r, g3_s, g3_r, w1_s, w1_r, w2_s, w2_r, wm_s, wm_r, wl_s,
    ra_s, ra_r, ry_s, ry_r,
):
    p = Place()
    s, t = p.s, p.t
    frame = jnp.bitwise_xor(s, t)
    origin = t == 0

    def rows_of(i):
        return pl.ds(pl.multiple_of(i * BLK, BLK), BLK)

    def tell(sem, dev):
        pl.semaphore_signal(sem, inc=1, device_id=dev, device_id_type=pl.DeviceIdType.MESH)

    inward = [
        pltpu.make_async_copy(src, dst, wl_s.at[j])
        for j, (src, dst) in enumerate(
            (
                (tok_h, tok_t),
                (mod_h, mod),
                (wout1_h, wout1),
                (wout2_h, wout2),
                (wqkv1_h, wqkv1),
                (wqkv2_h, wqkv2),
                (wmi_h, wia.at[0]),
                (wmo_h, woa.at[0]),
            )
        )
    ]
    for copy in inward:
        copy.start()

    barrier = pltpu.get_barrier_semaphore()
    x_peers = [(p.zh * 4 + lax.rem(p.x + j, 4), t) for j in (1, 2, 3)]
    z_peers = [(lax.rem(p.zh + j, 4) * 4 + p.x, t) for j in (1, 2, 3)]

    for dev in x_peers + z_peers + [p.z_outer()]:
        tell(barrier, dev)

    @pl.loop(1, N)
    def _(i):
        tell(barrier, (s, lax.rem(t + i, N)))

    inward[0].wait()
    rows = jnp.transpose(tok_t[...].astype(F32)).astype(BF)
    for k in range(N):
        pack(tok, k, rows[k * BLK:(k + 1) * BLK, :])
    pl.semaphore_wait(barrier, 22)

    def tok_copy(i):
        peer = lax.rem(t + i, N)
        return remote(tok.at[peer], tokr.at[t], tr_s.at[i], tr_r.at[t], (s, peer))

    @pl.loop(1, N)
    def _(i):
        tok_copy(i).start()

    tokr[t] = tok[t]
    for dev in x_peers:
        tell(known_x, dev)

    for copy in inward[1:6]:
        copy.wait()
    gw1 = WeightGather(wo1, w1_s, w1_r, p)
    gw2 = WeightGather(wo2, w2_s, w2_r, p)
    for w_in, w_all in ((wout1, wo1), (wout2, wo2)):
        w_all[t, 0:HD, :] = w_in[...]
        w_all[t, HD:PADW, :] = jnp.zeros((PADW - HD, D), BF)
    for copy in inward[6:]:
        copy.wait()
    mlp_copies = Copies(wm_s)

    def mlp_parts(parts):
        for low, size, outer in parts:
            for j, w_all in enumerate((wia, woa)):
                rows = pl.ds(low, size)
                sem = wm_r.at[j, low // 48]
                yield w_all.at[0, rows], w_all.at[1, rows], sem, p.z_outer() if outer else p.z_inner()

    def mlp_send(parts):
        for copy in mlp_parts(parts):
            mlp_copies.push(*copy)

    gw1.start_z()
    gw1.start_y(1)
    gw2.start_z()
    mlp_send(MLP_PARTS[:1])

    @pl.loop(1, N)
    def _(i):
        k = lax.rem(t + i, N)
        remote(tok.at[0], tokr.at[k], tr_s.at[0], tr_r.at[k], (s, k)).wait_recv()

    def side_by_side(blocks):
        for k in range(N):
            unpack(xb, 0, k * HD, blocks, k)

    side_by_side(tokr)
    x0b[...] = xb[...].astype(BF)
    ga1 = Gather(g1, g1_s, g1_r, p, 2, 3)
    g1[rows_of(t), :] = modulated(xb[...], mod[0:1, :], mod[1:2, :])
    ga1.start()
    wc1[...] = jnp.concatenate([wqkv1[j].astype(F32) for j in range(3)], axis=0).astype(BF)
    lanes = lax.broadcasted_iota(jnp.int32, (ROWS, 128), 1)
    vb[...] = jnp.where(lanes == HD, 1.0, 0.0).astype(BF)
    pl.semaphore_wait(known_x, 3)
    for dev in z_peers:
        tell(known_z, dev)
    ga1.forward()
    gw1.start_y(0)
    ga1.relay()
    pl.semaphore_wait(known_z, 3)

    def far_copy(src, dst, ss, rs, r):
        return remote(
            src.at[r], dst.at[t], ss.at[r], rs.at[t], (r, jnp.bitwise_xor(s, r))
        )

    def far_start(src, dst, ss, rs, r):
        own = jnp.logical_and(origin, r == s)

        @pl.when(jnp.logical_not(own))
        def _():
            far_copy(src, dst, ss, rs, r).start()

        @pl.when(own)
        def _():
            dst[t] = src[s]

    def far_wait_recv(src, dst, ss, rs):
        @pl.loop(0, N)
        def _(i):
            k = lax.rem(t + i, N)

            @pl.when(jnp.logical_not(jnp.logical_and(origin, i == 0)))
            def _():
                remote(
                    src.at[0], dst.at[k], ss.at[0], rs.at[k], p.partner()
                ).wait_recv()

    def far_wait_send(src, dst, ss, rs):
        @pl.loop(0, N)
        def _(r):
            @pl.when(jnp.logical_not(jnp.logical_and(origin, r == s)))
            def _():
                far_copy(src, dst, ss, rs, r).wait_send()

    corner = jnp.logical_and(s == 0, t == 0)
    row_copy = remote(x0b, x0f, tf_s, tf_r, (t, frame))

    @pl.when(jnp.logical_not(corner))
    def _():
        row_copy.start()

    @pl.when(corner)
    def _():
        x0f[...] = x0b[...]

    ga1.complete()

    @pl.loop(0, 3)
    def _(i):
        rows = pl.ds(pl.multiple_of(i * 256, 256), 256)
        r = dot_nt(g1[rows, :], wc1[...])
        qb[rows, :] = r[:, 0:HD].astype(BF)
        kb[rows, :] = r[:, HD:2 * HD].astype(BF)
        vb[rows, 0:HD] = r[:, 2 * HD:3 * HD].astype(BF)

    @pl.loop(0, 4)
    def _(i):
        ahead = jnp.where(i == 0, 2, jnp.where(i == 1, 1, jnp.where(i == 2, 3, 0)))
        part = lax.rem(p.zh + ahead, 4)
        rows = pl.ds(pl.multiple_of(part * 192, 192), 192)
        scores = dot_nt(qb[rows, :], kb[...])
        top = jnp.max(scores, axis=1, keepdims=True)
        raised = jnp.exp((scores - top) * SCALE).astype(BF)
        mixed = jnp.dot(raised, vb[...], preferred_element_type=F32)
        mixed = (mixed[:, 0:HD] / mixed[:, HD:HD + 1]).astype(BF)
        for j in range(4):
            pack(o1b, part * 4 + j, mixed[j * BLK:(j + 1) * BLK, :])
        for j in (2, 1, 3, 0):
            far_start(o1b, o1f, o1_s, o1_r, part * 4 + lax.rem(p.x + j, 4))

    gw2.start_y(1)
    gw2.start_y(0)
    gw1.forward()
    wc2[...] = jnp.concatenate([wqkv2[j].astype(F32) for j in range(3)], axis=0).astype(BF)
    xp[...] = jnp.zeros((BLK, N * PADW), F32)
    @pl.when(jnp.logical_not(corner))
    def _():
        row_copy.wait_recv()

    gw1.relay()
    far_wait_recv(o1b, o1f, o1_s, o1_r)
    gw1.complete()

    def project(blocks, weights):
        for k in range(N):
            unpack(xp, 0, k * PADW, blocks, k)
        return jnp.dot(
            xp[...].astype(BF), weights[...].reshape(N * PADW, D), preferred_element_type=F32
        )

    x1 = (x0f[...].astype(F32) + mod[2:3, :] * project(o1f, wo1)).astype(BF).astype(F32)
    xb[...] = x1
    ga2 = Gather(g2, g2_s, g2_r, p, 2, 3)
    g2[rows_of(t), :] = modulated(x1, mod[3:4, :], mod[4:5, :])
    ga2.start()
    ga2.forward()
    gw2.forward()
    ga2.relay()

    ga2.complete()

    @pl.loop(0, 3)
    def _(i):
        rows = pl.ds(pl.multiple_of(i * 256, 256), 256)
        qkvb[rows, :] = dot_nt(g2[rows, :], wc2[...]).astype(BF)

    same = lax.rem(lax.broadcasted_iota(jnp.int32, (256, 256), 0), 16) == lax.rem(
        lax.broadcasted_iota(jnp.int32, (256, 256), 1), 16
    )
    for grp in range(3):
        part = jnp.concatenate(
            [qkvb[f * BLK + grp * 16:f * BLK + grp * 16 + 16, :] for f in range(N)], axis=0
        )
        q, k, v = part[:, 0:HD], part[:, HD:2 * HD], part[:, 2 * HD:3 * HD]
        scores = jnp.where(same, dot_nt(q, k), -1e30)
        top = jnp.max(scores, axis=1, keepdims=True)
        raised = jnp.where(same, jnp.exp((scores - top) * SCALE), 0.0)
        weights = (raised / jnp.sum(raised, axis=1, keepdims=True)).astype(BF)
        mixed = jnp.dot(weights, v, preferred_element_type=F32).astype(BF)
        for f in range(N):
            o2b[f * BLK + grp * 16:f * BLK + grp * 16 + 16, :] = mixed[f * 16:f * 16 + 16, :]

    for f in range(N):
        pack(o2p, f, o2b[f * BLK:(f + 1) * BLK, :])

    def o2_copy(i):
        peer = lax.rem(t + i, N)
        return remote(o2p.at[peer], o2r.at[t], o2_s.at[i], o2_r.at[t], (s, peer))

    @pl.loop(1, N)
    def _(i):
        o2_copy(i).start()

    o2r[t] = o2p[t]
    mlp_send(MLP_PARTS[1:])
    gw2.relay()

    @pl.loop(1, N)
    def _(i):
        k = lax.rem(t + i, N)
        remote(o2p.at[0], o2r.at[k], o2_s.at[0], o2_r.at[k], (s, k)).wait_recv()

    gw2.complete()
    x2 = (xb[...] + mod[5:6, :] * project(o2r, wo2)).astype(BF).astype(F32)
    xb[...] = x2
    ga3 = Gather(g3, g3_s, g3_r, p, 1, 3)
    g3[rows_of(lax.rem(t, 8)), :] = modulated(x2, mod[6:7, :], mod[7:8, :])
    ga3.start()
    for src, dst, sem, _ in mlp_parts(MLP_PARTS):
        remote(src, dst, wm_s.at[0], sem, p.partner()).wait_recv()
    ga3.relay()
    ga3.complete()

    def mlp(cc):
        rows = jnp.concatenate([g3[rows_of(yy * 2 + cc), :] for yy in range(4)], axis=0)
        total = None
        for h in range(2):
            hidden = jax.nn.gelu(dot_nt(rows, wia[h]), approximate=True).astype(BF)
            term = jnp.dot(hidden, woa[h], preferred_element_type=F32)
            total = term if total is None else total + term
        return total

    def ra_copy(j):
        return remote(rs_send.at[j], rs_a.at[j], ra_s.at[j], ra_r.at[j], p.partner())

    r = mlp(1 - p.c)
    for yy in range(4):
        rs_send[yy] = r[yy * BLK:(yy + 1) * BLK, :].astype(BF)
        ra_copy(yy).start()
    r = mlp(p.c)
    for yy in range(4):
        own_sum[yy] = r[yy * BLK:(yy + 1) * BLK, :]

    def chip_sum(yy):
        ra_copy(yy).wait_recv()
        return own_sum[yy] + rs_a[yy].astype(F32)

    def ry_copy(j, yy):
        return remote(mid.at[j], rs_y.at[j], ry_s.at[j], ry_r.at[j], p.dev(p.z, yy, p.c))

    ring = (p.far, p.up, p.down)
    for j, yy in enumerate(ring):
        mid[j] = chip_sum(yy).astype(BF)
        ry_copy(j, yy).start()
    total = chip_sum(p.y)
    for j, yy in enumerate(ring):
        ry_copy(j, yy).wait_recv()
        total = total + rs_y[j].astype(F32)
    result = (xb[...] + mod[8:9, :] * total).astype(BF)
    for k in range(N):
        pack(res_s, k, result[:, k * HD:(k + 1) * HD])

    def res_copy(i):
        k = lax.rem(t + i, N)
        return remote(res_s.at[k], res_r.at[s], re_s.at[i], re_r.at[s], (frame, k))

    @pl.when(jnp.logical_not(origin))
    def _():
        res_copy(0).start()

    @pl.when(origin)
    def _():
        res_r[s] = res_s[t]

    @pl.loop(1, N)
    def _(i):
        res_copy(i).start()

    @pl.loop(1, N)
    def _(i):
        tok_copy(i).wait_send()
        o2_copy(i).wait_send()

    @pl.when(jnp.logical_not(corner))
    def _():
        row_copy.wait_send()

    far_wait_send(o1b, o1f, o1_s, o1_r)
    for g in (ga1, ga2, ga3, gw1, gw2):
        g.copies.finish()
    mlp_copies.finish()
    for yy in range(4):
        ra_copy(yy).wait_send()
    for j, yy in enumerate(ring):
        ry_copy(j, yy).wait_send()

    @pl.when(jnp.logical_not(origin))
    def _():
        res_copy(0).wait_send()
        remote(res_s.at[0], res_r.at[s], re_s.at[0], re_r.at[s], p.partner()).wait_recv()

    @pl.loop(1, N)
    def _(i):
        res_copy(i).wait_send()
        k = lax.rem(s + i, N)
        remote(res_s.at[0], res_r.at[k], re_s.at[0], re_r.at[k], p.partner()).wait_recv()

    for k in range(N):
        unpack(rows_f, k * BLK, 0, res_r, k)
    out_t[...] = jnp.transpose(rows_f[...]).astype(BF)


def per_device(tokens, modulation, spatial_qkv, spatial_out, temporal_qkv, temporal_out, mlp_in, mlp_out):
    vm = pltpu.VMEM
    dma = pltpu.SemaphoreType.DMA
    regular = pltpu.SemaphoreType.REGULAR
    scratch = [
        vm((HD, ROWS), BF),
        vm((9, D), F32),
        vm((3, HD, D), BF),
        vm((HD, D), BF),
        vm((3, HD, D), BF),
        vm((HD, D), BF),
        vm((N, PK, 128), BF),
        vm((N, PK, 128), BF),
        vm((BLK, D), BF),
        vm((BLK, D), BF),
        vm((ROWS, D), BF),
        vm((ROWS, D), BF),
        vm((ROWS // 2, D), BF),
        vm((N, PADW, D), BF),
        vm((N, PADW, D), BF),
        vm((3 * HD, D), BF),
        vm((3 * HD, D), BF),
        vm((2, FFL, D), BF),
        vm((2, FFL, D), BF),
        vm((ROWS, HD), BF),
        vm((ROWS, HD), BF),
        vm((ROWS, 128), BF),
        vm((N, PK, 128), BF),
        vm((N, PK, 128), BF),
        vm((ROWS, 3 * HD), BF),
        vm((ROWS, HD), BF),
        vm((N, PK, 128), BF),
        vm((N, PK, 128), BF),
        vm((BLK, D), F32),
        vm((BLK, N * PADW), F32),
        vm((ROWS, HD), F32),
        vm((4, BLK, D), BF),
        vm((4, BLK, D), BF),
        vm((4, BLK, D), F32),
        vm((3, BLK, D), BF),
        vm((3, BLK, D), BF),
        vm((N, PK, 128), BF),
        vm((N, PK, 128), BF),
        regular,
        regular,
    ]
    scratch += [dma((N,))] * 2 + [dma, dma] + [dma((N,))] * 6
    scratch += [dma((64,)), dma((N, 3))] * 3
    scratch += [dma((24,)), dma((N, 2))] * 2
    scratch += [dma((6,)), dma((2, 6)), dma((8,))]
    scratch += [dma((4,)), dma((4,)), dma((3,)), dma((3,))]
    return pl.pallas_call(
        kernel,
        out_shape=jax.ShapeDtypeStruct((HD, ROWS), BF),
        in_specs=[pl.BlockSpec(memory_space=pltpu.HBM)] * 8,
        out_specs=pl.BlockSpec(memory_space=pltpu.VMEM),
        scratch_shapes=scratch,
        compiler_params=pltpu.CompilerParams(
            collective_id=0, has_side_effects=True, vmem_limit_bytes=60 * 1024 * 1024
        ),
        cost_estimate=pl.CostEstimate(
            flops=2_300_000_000, bytes_accessed=4_000_000, transcendentals=1_000_000
        ),
    )(
        tokens.T,
        modulation,
        jnp.swapaxes(spatial_qkv, 1, 2),
        spatial_out,
        jnp.swapaxes(temporal_qkv, 1, 2),
        temporal_out,
        mlp_in.T,
        mlp_out,
    ).T


def solution(mesh):
    return jax.shard_map(
        per_device,
        mesh=mesh,
        in_specs=(
            P("seq", "tp"),
            P(),
            P(None, None, "tp"),
            P("tp", None),
            P(None, None, "tp"),
            P("tp", None),
            P(None, "tp"),
            P("tp", None),
        ),
        out_specs=P("seq", "tp"),
        check_vma=False,
    )
```
